32 devices in a mesh: head: 4 (over x, core), blk: 8 (over z, y).
Axes of the slice: x: 2, y: 2, z: 4, core: 2. Of those that a mesh axis runs over, the one named last changes fastest.
Arguments:
- queries: bfloat16 [6144, 32, 128], P(('blk', 'head')), may hold values from -6 to 6
- rotated_keys: bfloat16 [6144, 8, 128], P(('blk', 'head')), may hold values from -6 to 6
- value_vectors: bfloat16 [6144, 8, 128], P(('blk', 'head')), may hold values from -6 to 6
- block_list: int32 [8, 48, 8], replicated, may hold values from 0 to 47, as said below
- grad_out: bfloat16 [6144, 32, 128], P(('blk', 'head')), may hold values from -6 to 6
Outputs:
- attn_out: bfloat16 [6144, 32, 128], P(('blk', 'head'))
- grad_queries: bfloat16 [6144, 32, 128], P(('blk', 'head'))
- key_gradient: bfloat16 [6144, 8, 128], P(('blk', 'head'))
- value_gradient: bfloat16 [6144, 8, 128], P(('blk', 'head'))
The draws below stay inside these ranges and needn't reach their ends.
Inputs may be any that keep to these rules, and one draw needn't show every extreme that they name: Slot 0 of block_list[g, b, :] is b itself; every other slot names a distinct block below b or repeats b. For one head g, the blocks listed by the 6 query blocks of a run (blocks r * 6 to (r + 1) * 6 - 1) lie in that run or, for each earlier run, in one single block of it; the last query block of every run but the first lists a block of the run before.
All inputs are finite; a program needn't handle non-finite values.
Results may differ from the reference program's by a relative error of at most 0.035.
Values may be sent and summed in bfloat16 or wider, within the bound.
A program may use at most 192 MiB of HBM per device.

```python
import jax
import jax.numpy as jnp
from jax import lax

QUERY_HEADS = 32
KEY_HEADS = 8
HEAD_SIZE = 128
BLOCK_TOKENS = 128
TOPK = 8
SEQUENCE_TOKENS = 6144
RUN_BLOCKS = 6
SEQUENCE_BLOCKS = 48


def draw_queries(key, part):
    array_shape = (SEQUENCE_TOKENS, QUERY_HEADS, HEAD_SIZE)
    base_key = jax.random.fold_in(key, 11)
    base = jnp.clip(jax.random.normal(base_key, array_shape, jnp.float32), -5.0, 5.0)
    return base.astype(jnp.bfloat16)


def draw_rotated_keys(key, part):
    array_shape = (SEQUENCE_TOKENS, KEY_HEADS, HEAD_SIZE)
    base_key = jax.random.fold_in(key, 21)
    base = jnp.clip(jax.random.normal(base_key, array_shape, jnp.float32), -5.0, 5.0)
    return base.astype(jnp.bfloat16)


def draw_block_list(key, part):
    count_runs = SEQUENCE_BLOCKS // RUN_BLOCKS
    pool_random_key = jax.random.fold_in(key, 31)
    score_random_key = jax.random.fold_in(key, 32)
    run_index = jnp.arange(count_runs, dtype=jnp.int32)
    block_pool = run_index[None, None, :] * RUN_BLOCKS + jax.random.randint(pool_random_key, (KEY_HEADS, count_runs, count_runs), 0, RUN_BLOCKS)
    block_ids = jnp.arange(SEQUENCE_BLOCKS, dtype=jnp.int32)
    block_run = block_ids // RUN_BLOCKS
    pool_rows = block_pool[:, block_run, :]
    pool_hit = pool_rows[:, :, block_run] == block_ids[None, None, :]
    same_run = block_run[None, :] == block_run[:, None]
    valid = (block_ids[None, :] < block_ids[:, None])[None] & (same_run[None] | pool_hit)
    forced = ((block_ids % RUN_BLOCKS == RUN_BLOCKS - 1)[:, None] & (block_run[None, :] == block_run[:, None] - 1))[None] & pool_hit
    unsorted_draws = jax.random.randint(score_random_key, (KEY_HEADS, SEQUENCE_BLOCKS, SEQUENCE_BLOCKS), 0, 65536)
    score = jnp.where(forced, 2 ** 30, jnp.where(valid, unsorted_draws * SEQUENCE_BLOCKS + block_ids[None, None, :], -1))
    top_vals, picks = lax.top_k(score, TOPK - 1)
    chosen = jnp.where(top_vals >= 0, picks, block_ids[None, :, None])
    self_block = jnp.broadcast_to(block_ids[None, :, None], (KEY_HEADS, SEQUENCE_BLOCKS, 1))
    return jnp.concatenate([self_block, chosen], axis=-1).astype(jnp.int32)


def steps_of(key, extent, pieces, smallest, largest):
    gain = 1.0
    for dim, shards_of in pieces:
        draws = jax.random.uniform(jax.random.fold_in(jax.random.fold_in(key, 6), dim), (shards_of,), jnp.float32, smallest / len(pieces), largest / len(pieces))
        gain = gain * jnp.repeat(jnp.exp(draws), extent[dim] // shards_of).reshape((-1,) + (1,) * (len(extent) - 1 - dim))
    return gain


def scatter_about(rng, extent, width, bound, shards=(), kind=jnp.bfloat16):
    gain = steps_of(rng, extent, shards, -0.22, 0.18) if shards else 1.0
    array = jax.random.normal(rng, extent, jnp.float32) * width * gain
    return jnp.minimum(jnp.maximum(array, -bound), bound).astype(kind)


def setup_inputs(seed: int = 0) -> dict:
    splits = jax.random.split(jax.random.key(seed), 6)
    return {
        "queries": draw_queries(jax.random.fold_in(splits[5], 71), 0),
        "rotated_keys": draw_rotated_keys(jax.random.fold_in(splits[5], 71), 0),
        "value_vectors": scatter_about(splits[2], (SEQUENCE_TOKENS, KEY_HEADS, HEAD_SIZE), 1.0, 6.0, ((0, 32),)),
        "block_list": draw_block_list(jax.random.fold_in(splits[5], 71), 0),
        "grad_out": scatter_about(splits[4], (SEQUENCE_TOKENS, QUERY_HEADS, HEAD_SIZE), 1.0, 6.0, ((0, 32),)),
    }


def reference(queries, rotated_keys, value_vectors, block_list, grad_out):
    score_scale = HEAD_SIZE ** -0.5
    group_width = QUERY_HEADS // KEY_HEADS
    count_runs = SEQUENCE_BLOCKS // RUN_BLOCKS
    run_len = RUN_BLOCKS * BLOCK_TOKENS
    key_block_rows = rotated_keys.reshape(SEQUENCE_BLOCKS, BLOCK_TOKENS, KEY_HEADS, HEAD_SIZE)
    value_block_rows = value_vectors.reshape(SEQUENCE_BLOCKS, BLOCK_TOKENS, KEY_HEADS, HEAD_SIZE)
    group_index = jnp.arange(KEY_HEADS, dtype=jnp.int32)[:, None, None]
    slot_ids = jnp.arange(TOPK, dtype=jnp.int32)
    earlier = slot_ids[None, :] < slot_ids[:, None]
    offsets = jnp.arange(BLOCK_TOKENS, dtype=jnp.int32)

    def one_run(running_totals, run):
        key_total, value_total = running_totals
        first = (run * run_len).astype(jnp.int32)
        run_query = lax.dynamic_slice_in_dim(queries, first, run_len, 0).astype(jnp.float32)
        run_query = run_query.reshape(RUN_BLOCKS, BLOCK_TOKENS, KEY_HEADS, group_width, HEAD_SIZE)
        run_gradient = lax.dynamic_slice_in_dim(grad_out, first, run_len, 0).astype(jnp.float32)
        run_gradient = run_gradient.reshape(RUN_BLOCKS, BLOCK_TOKENS, KEY_HEADS, group_width, HEAD_SIZE)
        listed = lax.dynamic_slice_in_dim(block_list, (run * RUN_BLOCKS).astype(jnp.int32), RUN_BLOCKS, 1)
        keys_sel = key_block_rows[listed, :, group_index].astype(jnp.float32)
        values_sel = value_block_rows[listed, :, group_index].astype(jnp.float32)
        repeated = jnp.any((listed[..., :, None] == listed[..., None, :]) & earlier, axis=-1)
        query_pos = (run * RUN_BLOCKS + jnp.arange(RUN_BLOCKS, dtype=jnp.int32))[:, None] * BLOCK_TOKENS + offsets
        key_pos = listed[..., None] * BLOCK_TOKENS + offsets
        allowed = (key_pos[:, :, None, :, :] <= query_pos[None, :, :, None, None]) & jnp.logical_not(repeated)[:, :, None, :, None]
        scores = jnp.einsum('nqgjd,gnktd->gnqjkt', run_query, keys_sel) * score_scale
        scores = jnp.where(allowed[:, :, :, None], scores, -jnp.inf)
        row_max = jnp.max(scores, axis=(-2, -1), keepdims=True)
        log_total = row_max + jnp.log(jnp.sum(jnp.exp(scores - row_max), axis=(-2, -1), keepdims=True))
        probs = jnp.exp(scores - log_total)
        probs_b = lax.optimization_barrier(probs.astype(jnp.bfloat16)).astype(jnp.float32)
        output = jnp.einsum('gnqjkt,gnktd->nqgjd', probs_b, values_sel)
        output_b = output.astype(jnp.bfloat16)
        row_dot = jnp.sum(run_gradient * output_b.astype(jnp.float32), axis=-1)
        grad_probs = jnp.einsum('nqgjd,gnktd->gnqjkt', run_gradient, values_sel)
        grad_scores = probs * (grad_probs - jnp.transpose(row_dot, (2, 0, 1, 3))[..., None, None])
        grad_scores_b = lax.optimization_barrier(grad_scores.astype(jnp.bfloat16)).astype(jnp.float32)
        query_grad = (jnp.einsum('gnqjkt,gnktd->nqgjd', grad_scores_b, keys_sel) * score_scale).astype(jnp.bfloat16)
        key_slots = jnp.einsum('gnqjkt,nqgjd->gnktd', grad_scores_b, run_query) * score_scale
        value_slots = jnp.einsum('gnqjkt,nqgjd->gnktd', probs_b, run_gradient)
        complete_zeros = jnp.zeros((SEQUENCE_BLOCKS, KEY_HEADS, BLOCK_TOKENS, HEAD_SIZE), jnp.float32)
        key_part = complete_zeros.at[listed, group_index].add(key_slots)
        value_part = complete_zeros.at[listed, group_index].add(value_slots)
        key_part = lax.optimization_barrier(key_part.astype(jnp.bfloat16)).astype(jnp.float32)
        value_part = lax.optimization_barrier(value_part.astype(jnp.bfloat16)).astype(jnp.float32)
        return (key_total + key_part, value_total + value_part), (output_b.reshape(run_len, QUERY_HEADS, HEAD_SIZE), query_grad.reshape(run_len, QUERY_HEADS, HEAD_SIZE))

    initial_totals = (jnp.zeros((SEQUENCE_BLOCKS, KEY_HEADS, BLOCK_TOKENS, HEAD_SIZE), jnp.float32), jnp.zeros((SEQUENCE_BLOCKS, KEY_HEADS, BLOCK_TOKENS, HEAD_SIZE), jnp.float32))
    running_totals, results = lax.scan(one_run, initial_totals, jnp.arange(count_runs, dtype=jnp.int32))
    attn_out = results[0].reshape(SEQUENCE_TOKENS, QUERY_HEADS, HEAD_SIZE)
    grad_queries = results[1].reshape(SEQUENCE_TOKENS, QUERY_HEADS, HEAD_SIZE)
    key_gradient = jnp.transpose(running_totals[0], (0, 2, 1, 3)).reshape(SEQUENCE_TOKENS, KEY_HEADS, HEAD_SIZE).astype(jnp.bfloat16)
    value_gradient = jnp.transpose(running_totals[1], (0, 2, 1, 3)).reshape(SEQUENCE_TOKENS, KEY_HEADS, HEAD_SIZE).astype(jnp.bfloat16)
    return attn_out, grad_queries, key_gradient, value_gradient
```

```python
import functools

import jax
import jax.numpy as jnp
from jax import lax
from jax.experimental import pallas as pl
from jax.experimental.pallas import tpu as pltpu
from jax.sharding import PartitionSpec as P

BLOCK = 128
TOPK = 8
LOG2E = 1.4426950408889634
MESH = pl.DeviceIdType.MESH
VMEM_LIMIT = 56 * 1024 * 1024


def greet(heads, peers):
    me = lax.axis_index("head")
    rank = lax.axis_index("blk")
    barrier = pltpu.get_barrier_semaphore()
    for d in range(1, heads):
        pl.semaphore_signal(
            barrier, inc=1, device_id=(lax.rem(me + d, heads), rank), device_id_type=MESH
        )
    for d in range(1, peers):
        pl.semaphore_signal(
            barrier, inc=1, device_id=(me, lax.rem(rank + d, peers)), device_id_type=MESH
        )
    pl.semaphore_wait(barrier, heads + peers - 2)
    return me, rank


def bring_kernel(
    heads, peers, groups, run_blocks,
    named, q_ref, do_ref, k_ref, v_ref,
    qh_ref, doh_ref, kv_ref, recv_ref,
    stage, own_sem, head_send, head_recv, blk_send, blk_recv,
):
    me, rank = greet(heads, peers)
    tokens = k_ref.shape[1]
    rows = q_ref.shape[1]

    def pieces(dest):
        part = pl.ds(dest * groups, groups)
        return (
            (k_ref.at[part], kv_ref.at[0, :, pl.ds(pl.multiple_of(me * tokens, 64), tokens)]),
            (v_ref.at[part], kv_ref.at[1, :, pl.ds(pl.multiple_of(me * tokens, 64), tokens)]),
            (q_ref.at[part], qh_ref.at[:, pl.ds(pl.multiple_of(me * rows, 128), rows)]),
            (do_ref.at[part], doh_ref.at[:, pl.ds(pl.multiple_of(me * rows, 128), rows)]),
        )

    remote = {}
    local = []
    for n in range(4):
        for d in range(1, heads):
            dest = lax.rem(me + d, heads)
            src, dst = pieces(dest)[n]
            copy = pltpu.make_async_remote_copy(
                src_ref=src, dst_ref=dst,
                send_sem=head_send.at[n, d], recv_sem=head_recv.at[n, d],
                device_id=(dest, rank), device_id_type=MESH,
            )
            copy.start()
            remote[n, d] = copy
        src, dst = pieces(me)[n]
        copy = pltpu.make_async_copy(src, dst, own_sem.at[n])
        copy.start()
        local.append(copy)
    for n in range(2):
        local[n].wait()
        for d in range(1, heads):
            remote[n, d].wait_recv()
    blk_copies = []
    for d in range(1, peers):
        peer = lax.rem(rank + d, peers)
        for g in range(groups):
            block = named[g * peers + peer]
            for n in range(2):
                total = jnp.zeros((BLOCK, kv_ref.shape[-1]), jnp.float32)
                for i in range(run_blocks):
                    weight = (block == i).astype(jnp.float32)
                    piece = kv_ref[n, g, i * BLOCK : (i + 1) * BLOCK, :]
                    total = total + weight * piece.astype(jnp.float32)
                stage[d, n, g] = total.astype(jnp.bfloat16)
        copy = pltpu.make_async_remote_copy(
            src_ref=stage.at[d], dst_ref=recv_ref.at[rank],
            send_sem=blk_send.at[d], recv_sem=blk_recv.at[d],
            device_id=(me, peer), device_id_type=MESH,
        )
        copy.start()
        blk_copies.append(copy)
    for n in range(2, 4):
        local[n].wait()
        for d in range(1, heads):
            remote[n, d].wait_recv()
    for copy in remote.values():
        copy.wait_send()
    for copy in blk_copies:
        copy.wait()


def attend_kernel(
    run_blocks, seq_blocks,
    place, lists, q_ref, do_ref, kv_ref, recv_ref,
    out_ref, dq_ref, own_ref, far_ref,
    k_buf, v_buf, acc_own, acc_far,
):
    g, b = pl.program_id(0), pl.program_id(1)
    groups = pl.num_programs(0)
    base = place[1] * run_blocks
    scale = q_ref.shape[-1] ** -0.5
    width = q_ref.shape[1] // BLOCK

    @pl.when(b == 0)
    def _():
        acc_own[...] = jnp.zeros_like(acc_own)
        acc_far[...] = jnp.zeros_like(acc_far)

    first = ((place[0] * groups + g) * seq_blocks + base + b) * TOPK
    slots = []
    for s in range(TOPK):
        listed = lists[first + s]
        mine = listed >= base
        at = jnp.clip(listed - base, 0, run_blocks - 1)
        owner = listed // run_blocks
        slots.append((listed, mine, at, owner))

        @pl.when(mine)
        def _():
            rows = pl.ds(pl.multiple_of(at * BLOCK, BLOCK), BLOCK)
            k_buf[s * BLOCK : (s + 1) * BLOCK] = kv_ref[0, g, rows, :]
            v_buf[s * BLOCK : (s + 1) * BLOCK] = kv_ref[1, g, rows, :]

        @pl.when(jnp.logical_not(mine))
        def _():
            k_buf[s * BLOCK : (s + 1) * BLOCK] = recv_ref[owner, 0, g]
            v_buf[s * BLOCK : (s + 1) * BLOCK] = recv_ref[owner, 1, g]

    q, do = q_ref[0], do_ref[0]
    keys, values = k_buf[...], v_buf[...]
    across = (((1,), (1,)), ((), ()))
    f32 = jnp.float32
    scores = lax.dot_general(keys, q, across, preferred_element_type=f32)
    shape = (BLOCK, q.shape[0])
    causal = lax.broadcasted_iota(jnp.int32, shape, 0) * width <= lax.broadcasted_iota(
        jnp.int32, shape, 1
    )
    parts = [jnp.where(causal, scores[:BLOCK], -1e30)]
    for s in range(1, TOPK):
        parts.append(
            jnp.where(slots[s][0] != base + b, scores[s * BLOCK : (s + 1) * BLOCK], -1e30)
        )
    scores = jnp.concatenate(parts, axis=0)
    top = jnp.max(scores, axis=0, keepdims=True)
    weights = jnp.exp2((scores - top) * (scale * LOG2E))
    probs = weights * (1.0 / jnp.sum(weights, axis=0, keepdims=True))
    probs_b = probs.astype(jnp.bfloat16)
    out_t = lax.dot_general(values.T, probs_b, (((1,), (0,)), ((), ())), preferred_element_type=f32)
    out_b = out_t.T.astype(jnp.bfloat16)
    out_ref[0] = out_b
    row_dot = jnp.sum(
        do.astype(f32).T * out_t.astype(jnp.bfloat16).astype(f32), axis=0, keepdims=True
    )
    grad_probs = lax.dot_general(values, do, across, preferred_element_type=f32)
    grad_scores = (probs * (grad_probs - row_dot)).astype(jnp.bfloat16)
    dq_t = lax.dot_general(
        keys.T, grad_scores, (((1,), (0,)), ((), ())), preferred_element_type=f32
    )
    dq_ref[0] = (dq_t * scale).T.astype(jnp.bfloat16)
    dk = jnp.dot(grad_scores, q, preferred_element_type=f32)
    dv = jnp.dot(probs_b, do, preferred_element_type=f32)
    for s in range(TOPK):
        listed, mine, at, owner = slots[s]
        dk_s, dv_s = dk[s * BLOCK : (s + 1) * BLOCK], dv[s * BLOCK : (s + 1) * BLOCK]

        @pl.when(mine)
        def _():
            rows = pl.ds(pl.multiple_of(at * BLOCK, BLOCK), BLOCK)
            acc_own[0, rows, :] += dk_s
            acc_own[1, rows, :] += dv_s

        @pl.when(jnp.logical_not(mine))
        def _():
            acc_far[owner, 0] += dk_s
            acc_far[owner, 1] += dv_s

    @pl.when(b == run_blocks - 1)
    def _():
        own_ref[0, 0] = (acc_own[0] * scale).astype(jnp.bfloat16)
        own_ref[1, 0] = acc_own[1].astype(jnp.bfloat16)
        for j in range(acc_far.shape[0]):
            far_ref[j, 0, 0] = (acc_far[j, 0] * scale).astype(jnp.bfloat16)
            far_ref[j, 1, 0] = acc_far[j, 1].astype(jnp.bfloat16)


def return_kernel(
    heads, peers, groups, run_blocks,
    named, outh_ref, dqh_ref, own_ref, far_ref,
    out_ref, dq_ref, kv_ref,
    recv, stage, own_sem, head_send, head_recv, blk_send, blk_recv,
):
    me, rank = greet(heads, peers)
    rows = out_ref.shape[1]
    tokens = kv_ref.shape[2]
    blk_copies = []
    for d in range(1, peers):
        peer = lax.rem(rank + d, peers)
        copy = pltpu.make_async_remote_copy(
            src_ref=far_ref.at[peer], dst_ref=recv.at[rank],
            send_sem=blk_send.at[d], recv_sem=blk_recv.at[d],
            device_id=(me, peer), device_id_type=MESH,
        )
        copy.start()
        blk_copies.append(copy)

    def pieces(dest):
        part = pl.ds(me * groups, groups)
        here = pl.ds(pl.multiple_of(dest * rows, 128), rows)
        some = pl.ds(pl.multiple_of(dest * tokens, 64), tokens)
        return (
            (outh_ref.at[:, here], out_ref.at[part]),
            (dqh_ref.at[:, here], dq_ref.at[part]),
            (stage.at[:, :, some], kv_ref.at[:, part]),
        )

    copies = []

    def send(n):
        for d in range(1, heads):
            dest = lax.rem(me + d, heads)
            src, dst = pieces(dest)[n]
            copy = pltpu.make_async_remote_copy(
                src_ref=src, dst_ref=dst,
                send_sem=head_send.at[n, d], recv_sem=head_recv.at[n, d],
                device_id=(dest, rank), device_id_type=MESH,
            )
            copy.start()
            copies.append(copy)
        src, dst = pieces(me)[n]
        copy = pltpu.make_async_copy(src, dst, own_sem.at[n])
        copy.start()
        copies.append(copy)

    send(0)
    send(1)
    for copy in blk_copies:
        copy.wait()
    for g in range(groups):
        for n in range(2):
            def settle(i, _):
                at = pl.ds(pl.multiple_of(i * BLOCK, BLOCK), BLOCK)

                def add(d, total):
                    peer = lax.rem(rank + d, peers)
                    weight = (named[g * peers + peer] == i).astype(jnp.float32)
                    return total + weight * recv[peer, n, g].astype(jnp.float32)

                total = own_ref[n, g, at, :].astype(jnp.float32)
                total = lax.fori_loop(1, peers, add, total)
                stage[n, g, at, :] = total.astype(jnp.bfloat16)
                return 0

            lax.fori_loop(0, run_blocks, settle, 0)
    send(2)
    for copy in copies:
        copy.wait()


def on_device(queries, rotated_keys, value_vectors, block_list, grad_out):
    tokens, head_count, width = queries.shape
    group_count = rotated_keys.shape[1]
    per_group = head_count // group_count
    heads, peers = lax.axis_size("head"), lax.axis_size("blk")
    me, rank = lax.axis_index("head"), lax.axis_index("blk")
    groups = group_count // heads
    run_len = tokens * heads
    run_blocks = run_len // BLOCK
    seq_blocks = block_list.shape[1]
    rows = tokens * per_group
    bf16 = jnp.bfloat16

    def by_group(array):
        array = array.reshape(tokens, group_count, -1, width)
        return jnp.transpose(array, (1, 0, 2, 3)).reshape(group_count, -1, width)

    lists_here = lax.dynamic_slice_in_dim(block_list, me * groups, groups, 0)
    listing = lists_here.reshape(groups, peers, run_blocks * TOPK)
    inside = (listing // run_blocks == rank) & (jnp.arange(peers) != rank)[None, :, None]
    named = jnp.max(jnp.where(inside, listing - rank * run_blocks, -1), axis=2).reshape(-1)

    any_space = pl.BlockSpec(memory_space=pl.ANY)
    vmem = pl.BlockSpec(memory_space=pltpu.VMEM)
    smem = pl.BlockSpec(memory_space=pltpu.SMEM)
    dma = pltpu.SemaphoreType.DMA
    params = functools.partial(
        pltpu.CompilerParams, has_side_effects=True, vmem_limit_bytes=VMEM_LIMIT
    )
    far_shape = (peers, 2, groups, BLOCK, width)
    own_shape = (2, groups, run_len, width)
    q_shape = (groups, rows * heads, width)
    qh, doh, kv, recv = pl.pallas_call(
        functools.partial(bring_kernel, heads, peers, groups, run_blocks),
        out_shape=(
            jax.ShapeDtypeStruct(q_shape, bf16),
            jax.ShapeDtypeStruct(q_shape, bf16),
            jax.ShapeDtypeStruct(own_shape, bf16),
            jax.ShapeDtypeStruct(far_shape, bf16),
        ),
        in_specs=[smem] + [any_space] * 4,
        out_specs=(any_space, any_space, vmem, any_space),
        scratch_shapes=[
            pltpu.VMEM(far_shape, bf16),
            dma((4,)), dma((4, heads)), dma((4, heads)), dma((peers,)), dma((peers,)),
        ],
        compiler_params=params(collective_id=0),
        name="bring",
    )(named, by_group(queries), by_group(grad_out), by_group(rotated_keys), by_group(value_vectors))

    place = jnp.stack([me, rank]).astype(jnp.int32)
    item = pl.BlockSpec((1, BLOCK * per_group, width), lambda g, b, *_: (g, b, 0))
    outh, dqh, own, far = pl.pallas_call(
        functools.partial(attend_kernel, run_blocks, seq_blocks),
        grid_spec=pltpu.PrefetchScalarGridSpec(
            num_scalar_prefetch=2,
            grid=(groups, run_blocks),
            in_specs=[
                item, item,
                pl.BlockSpec(own_shape, lambda g, b, *_: (0, 0, 0, 0)),
                pl.BlockSpec(far_shape, lambda g, b, *_: (0, 0, 0, 0, 0)),
            ],
            out_specs=(
                item, item,
                pl.BlockSpec((2, 1, run_len, width), lambda g, b, *_: (0, g, 0, 0)),
                pl.BlockSpec((peers, 2, 1, BLOCK, width), lambda g, b, *_: (0, 0, g, 0, 0)),
            ),
            scratch_shapes=[
                pltpu.VMEM((TOPK * BLOCK, width), bf16),
                pltpu.VMEM((TOPK * BLOCK, width), bf16),
                pltpu.VMEM((2, run_len, width), jnp.float32),
                pltpu.VMEM((peers, 2, BLOCK, width), jnp.float32),
            ],
        ),
        out_shape=(
            jax.ShapeDtypeStruct(q_shape, bf16),
            jax.ShapeDtypeStruct(q_shape, bf16),
            jax.ShapeDtypeStruct(own_shape, bf16),
            jax.ShapeDtypeStruct(far_shape, bf16),
        ),
        compiler_params=pltpu.CompilerParams(
            dimension_semantics=("arbitrary", "arbitrary"), vmem_limit_bytes=VMEM_LIMIT
        ),
        name="attend",
    )(place, block_list.reshape(-1), qh, doh, kv, recv)

    out_g, dq_g, kv_g = pl.pallas_call(
        functools.partial(return_kernel, heads, peers, groups, run_blocks),
        out_shape=(
            jax.ShapeDtypeStruct((group_count, rows, width), bf16),
            jax.ShapeDtypeStruct((group_count, rows, width), bf16),
            jax.ShapeDtypeStruct((2, group_count, tokens, width), bf16),
        ),
        in_specs=[smem, any_space, any_space, vmem, any_space],
        out_specs=(any_space, any_space, any_space),
        scratch_shapes=[
            pltpu.VMEM(far_shape, bf16),
            pltpu.VMEM(own_shape, bf16),
            dma((3,)), dma((3, heads)), dma((3, heads)), dma((peers,)), dma((peers,)),
        ],
        compiler_params=params(collective_id=1),
        name="give_back",
    )(named, outh, dqh, own, far)

    def by_token(array, count):
        array = array.reshape(group_count, tokens, count, width)
        return jnp.transpose(array, (1, 0, 2, 3)).reshape(tokens, group_count * count, width)

    return (
        by_token(out_g, per_group),
        by_token(dq_g, per_group),
        by_token(kv_g[0], 1),
        by_token(kv_g[1], 1),
    )


def solution(mesh):
    split = P(("blk", "head"), None, None)
    return jax.shard_map(
        on_device,
        mesh=mesh,
        in_specs=(split, split, split, P(), split),
        out_specs=(split, split, split, split),
        check_vma=False,
    )
```

```python
import functools

import jax
import jax.numpy as jnp
from jax import lax
from jax.experimental import pallas as pl
from jax.experimental.pallas import tpu as pltpu
from jax.sharding import PartitionSpec as P

BLOCK = 128
TOPK = 8
LOG2E = 1.4426950408889634
MESH = pl.DeviceIdType.MESH
VMEM_LIMIT = 56 * 1024 * 1024


def greet(heads, peers):
    me = lax.axis_index("head")
    rank = lax.axis_index("blk")
    barrier = pltpu.get_barrier_semaphore()
    for d in range(1, heads):
        pl.semaphore_signal(
            barrier, inc=1, device_id=(lax.rem(me + d, heads), rank), device_id_type=MESH
        )
    for d in range(1, peers):
        pl.semaphore_signal(
            barrier, inc=1, device_id=(me, lax.rem(rank + d, peers)), device_id_type=MESH
        )
    pl.semaphore_wait(barrier, heads + peers - 2)
    return me, rank


def bring_kernel(
    heads, peers, groups, run_blocks,
    named, q_ref, do_ref, k_ref, v_ref,
    qh_ref, doh_ref, kv_ref, recv_ref,
    stage, own_sem, head_send, head_recv, blk_send, blk_recv,
):
    me, rank = greet(heads, peers)
    tokens = k_ref.shape[1]
    rows = q_ref.shape[1]

    def pieces(dest):
        part = pl.ds(dest * groups, groups)
        return (
            (k_ref.at[part], kv_ref.at[0, :, pl.ds(pl.multiple_of(me * tokens, 64), tokens)]),
            (v_ref.at[part], kv_ref.at[1, :, pl.ds(pl.multiple_of(me * tokens, 64), tokens)]),
            (q_ref.at[dest * groups], qh_ref.at[pl.ds(pl.multiple_of(me * rows, 128), rows)]),
            (do_ref.at[dest * groups], doh_ref.at[pl.ds(pl.multiple_of(me * rows, 128), rows)]),
        )

    remote = {}
    local = []
    for n in range(4):
        for d in range(1, heads):
            dest = lax.rem(me + d, heads)
            src, dst = pieces(dest)[n]
            copy = pltpu.make_async_remote_copy(
                src_ref=src, dst_ref=dst,
                send_sem=head_send.at[n, d], recv_sem=head_recv.at[n, d],
                device_id=(dest, rank), device_id_type=MESH,
            )
            copy.start()
            remote[n, d] = copy
        src, dst = pieces(me)[n]
        copy = pltpu.make_async_copy(src, dst, own_sem.at[n])
        copy.start()
        local.append(copy)
    for n in range(2):
        local[n].wait()
        for d in range(1, heads):
            remote[n, d].wait_recv()
    blk_copies = []
    for d in range(1, peers):
        peer = lax.rem(rank + d, peers)
        for g in range(groups):
            block = named[g * peers + peer]
            for n in range(2):
                total = jnp.zeros((BLOCK, kv_ref.shape[-1]), jnp.float32)
                for i in range(run_blocks):
                    weight = (block == i).astype(jnp.float32)
                    piece = kv_ref[n, g, i * BLOCK : (i + 1) * BLOCK, :]
                    total = total + weight * piece.astype(jnp.float32)
                stage[d, n, g] = total.astype(jnp.bfloat16)
        copy = pltpu.make_async_remote_copy(
            src_ref=stage.at[d], dst_ref=recv_ref.at[rank],
            send_sem=blk_send.at[d], recv_sem=blk_recv.at[d],
            device_id=(me, peer), device_id_type=MESH,
        )
        copy.start()
        blk_copies.append(copy)
    for n in range(2, 4):
        local[n].wait()
        for d in range(1, heads):
            remote[n, d].wait_recv()
    for copy in remote.values():
        copy.wait_send()
    for copy in blk_copies:
        copy.wait()


def attend_kernel(
    group, groups, run_blocks, seq_blocks,
    place, lists, q_ref, do_ref, kv_ref, recv_ref,
    od_ref, own_ref, far_ref,
    k_buf, v_buf, acc_own, acc_far,
):
    g, b = 0, pl.program_id(0)
    base = place[1] * run_blocks
    scale = q_ref.shape[-1] ** -0.5
    width = q_ref.shape[0] // BLOCK

    @pl.when(b == 0)
    def _():
        acc_own[...] = jnp.zeros_like(acc_own)
        acc_far[...] = jnp.zeros_like(acc_far)

    first = ((place[0] * groups + group) * seq_blocks + base + b) * TOPK
    slots = []
    for s in range(TOPK):
        listed = lists[first + s]
        mine = listed >= base
        at = jnp.clip(listed - base, 0, run_blocks - 1)
        owner = listed // run_blocks
        slots.append((listed, mine, at, owner))

        @pl.when(mine)
        def _():
            rows = pl.ds(pl.multiple_of(at * BLOCK, BLOCK), BLOCK)
            k_buf[s * BLOCK : (s + 1) * BLOCK] = kv_ref[0, g, rows, :]
            v_buf[s * BLOCK : (s + 1) * BLOCK] = kv_ref[1, g, rows, :]

        @pl.when(jnp.logical_not(mine))
        def _():
            k_buf[s * BLOCK : (s + 1) * BLOCK] = recv_ref[owner, 0, g]
            v_buf[s * BLOCK : (s + 1) * BLOCK] = recv_ref[owner, 1, g]

    q, do = q_ref[...], do_ref[...]
    keys, values = k_buf[...], v_buf[...]
    across = (((1,), (1,)), ((), ()))
    f32 = jnp.float32
    scores = lax.dot_general(keys, q, across, preferred_element_type=f32)
    shape = (BLOCK, q.shape[0])
    causal = lax.broadcasted_iota(jnp.int32, shape, 0) * width <= lax.broadcasted_iota(
        jnp.int32, shape, 1
    )
    parts = [jnp.where(causal, scores[:BLOCK], -1e30)]
    for s in range(1, TOPK):
        parts.append(
            jnp.where(slots[s][0] != base + b, scores[s * BLOCK : (s + 1) * BLOCK], -1e30)
        )
    scores = jnp.concatenate(parts, axis=0)
    top = jnp.max(scores, axis=0, keepdims=True)
    weights = jnp.exp2((scores - top) * (scale * LOG2E))
    probs = weights * (1.0 / jnp.sum(weights, axis=0, keepdims=True))
    probs_b = probs.astype(jnp.bfloat16)
    out_t = lax.dot_general(values.T, probs_b, (((1,), (0,)), ((), ())), preferred_element_type=f32)
    out_b = out_t.T.astype(jnp.bfloat16)
    od_ref[0] = out_b
    row_dot = jnp.sum(
        do.astype(f32).T * out_t.astype(jnp.bfloat16).astype(f32), axis=0, keepdims=True
    )
    grad_probs = lax.dot_general(values, do, across, preferred_element_type=f32)
    grad_scores = (probs * (grad_probs - row_dot)).astype(jnp.bfloat16)
    dq_t = lax.dot_general(
        keys.T, grad_scores, (((1,), (0,)), ((), ())), preferred_element_type=f32
    )
    od_ref[1] = (dq_t * scale).T.astype(jnp.bfloat16)
    dk = jnp.dot(grad_scores, q, preferred_element_type=f32)
    dv = jnp.dot(probs_b, do, preferred_element_type=f32)
    for s in range(TOPK):
        listed, mine, at, owner = slots[s]
        dk_s, dv_s = dk[s * BLOCK : (s + 1) * BLOCK], dv[s * BLOCK : (s + 1) * BLOCK]

        @pl.when(mine)
        def _():
            rows = pl.ds(pl.multiple_of(at * BLOCK, BLOCK), BLOCK)
            acc_own[0, rows, :] += dk_s
            acc_own[1, rows, :] += dv_s

        @pl.when(jnp.logical_not(mine))
        def _():
            acc_far[owner, 0] += dk_s
            acc_far[owner, 1] += dv_s

    @pl.when(b == run_blocks - 1)
    def _():
        own_ref[0] = (acc_own[0] * scale).astype(jnp.bfloat16)
        own_ref[1] = acc_own[1].astype(jnp.bfloat16)
        for j in range(acc_far.shape[0]):
            far_ref[j, 0] = (acc_far[j, 0] * scale).astype(jnp.bfloat16)
            far_ref[j, 1] = acc_far[j, 1].astype(jnp.bfloat16)


def return_kernel(
    heads, peers, groups, run_blocks, named, *refs,
):
    came, refs = refs[:heads], refs[heads:]
    last_refs, refs = refs[: groups - 1], refs[groups - 1 :]
    own_refs, refs = refs[:groups], refs[groups:]
    far_refs, refs = refs[:groups], refs[groups:]
    out_ref, dq_ref, kv_ref = refs[:3]
    recv, stage, own_sem, came_sem, head_send, head_recv, blk_send, blk_recv = refs[3:]
    me, rank = greet(heads, peers)
    rows = out_ref.shape[1]
    tokens = kv_ref.shape[2]
    blk_copies = []
    for d in range(1, peers):
        peer = lax.rem(rank + d, peers)
        for g in range(groups):
            copy = pltpu.make_async_remote_copy(
                src_ref=far_refs[g].at[peer], dst_ref=recv.at[rank, g],
                send_sem=blk_send.at[g, d], recv_sem=blk_recv.at[g, d],
                device_id=(me, peer), device_id_type=MESH,
            )
            copy.start()
            blk_copies.append(copy)

    def pieces(dest):
        here = pl.ds(pl.multiple_of(dest * rows, 128), rows)
        some = pl.ds(pl.multiple_of(dest * tokens, 64), tokens)
        pairs = []
        for g in range(1, groups):
            pairs.append((last_refs[g - 1].at[0, here], out_ref.at[me * groups + g]))
            pairs.append((last_refs[g - 1].at[1, here], dq_ref.at[me * groups + g]))
        pairs.append((stage.at[:, :, some], kv_ref.at[:, pl.ds(me * groups, groups)]))
        return pairs

    copies = []

    def send(n):
        for d in range(1, heads):
            dest = lax.rem(me + d, heads)
            src, dst = pieces(dest)[n]
            copy = pltpu.make_async_remote_copy(
                src_ref=src, dst_ref=dst,
                send_sem=head_send.at[n, d], recv_sem=head_recv.at[n, d],
                device_id=(dest, rank), device_id_type=MESH,
            )
            copy.start()
            copies.append(copy)
        src, dst = pieces(me)[n]
        copy = pltpu.make_async_copy(src, dst, own_sem.at[n])
        copy.start()
        copies.append(copy)

    last = 2 * (groups - 1)
    for n in range(last):
        send(n)
    for d in range(heads):
        source = lax.rem(me + heads - d, heads)
        for n, target in enumerate((out_ref, dq_ref)):
            copy = pltpu.make_async_copy(
                came[d].at[n], target.at[source * groups], came_sem.at[n, d]
            )
            copy.start()
            copies.append(copy)
    for copy in blk_copies:
        copy.wait()
    for g in range(groups):
        for n in range(2):
            def settle(i, _):
                at = pl.ds(pl.multiple_of(i * BLOCK, BLOCK), BLOCK)

                def add(d, total):
                    peer = lax.rem(rank + d, peers)
                    weight = (named[g * peers + peer] == i).astype(jnp.float32)
                    return total + weight * recv[peer, g, n].astype(jnp.float32)

                total = own_refs[g][n, at, :].astype(jnp.float32)
                total = lax.fori_loop(1, peers, add, total)
                stage[n, g, at, :] = total.astype(jnp.bfloat16)
                return 0

            lax.fori_loop(0, run_blocks, settle, 0)
    send(last)
    for copy in copies:
        copy.wait()


def on_device(queries, rotated_keys, value_vectors, block_list, grad_out):
    tokens, head_count, width = queries.shape
    group_count = rotated_keys.shape[1]
    per_group = head_count // group_count
    heads, peers = lax.axis_size("head"), lax.axis_size("blk")
    me, rank = lax.axis_index("head"), lax.axis_index("blk")
    groups = group_count // heads
    run_len = tokens * heads
    run_blocks = run_len // BLOCK
    seq_blocks = block_list.shape[1]
    rows = tokens * per_group
    bf16 = jnp.bfloat16

    def by_group(array):
        array = array.reshape(tokens, group_count, -1, width)
        return jnp.transpose(array, (1, 0, 2, 3)).reshape(group_count, -1, width)

    lists_here = lax.dynamic_slice_in_dim(block_list, me * groups, groups, 0)
    listing = lists_here.reshape(groups, peers, run_blocks * TOPK)
    inside = (listing // run_blocks == rank) & (jnp.arange(peers) != rank)[None, :, None]
    named = jnp.max(jnp.where(inside, listing - rank * run_blocks, -1), axis=2).reshape(-1)

    any_space = pl.BlockSpec(memory_space=pl.ANY)
    vmem = pl.BlockSpec(memory_space=pltpu.VMEM)
    smem = pl.BlockSpec(memory_space=pltpu.SMEM)
    dma = pltpu.SemaphoreType.DMA
    params = functools.partial(
        pltpu.CompilerParams, has_side_effects=True, vmem_limit_bytes=VMEM_LIMIT
    )
    far_shape = (peers, 2, groups, BLOCK, width)
    own_shape = (2, groups, run_len, width)
    q_shape = (rows * heads, width)
    q_t, do_t = by_group(queries), by_group(grad_out)
    qh, doh, kv, recv = pl.pallas_call(
        functools.partial(bring_kernel, heads, peers, groups, run_blocks),
        out_shape=(
            jax.ShapeDtypeStruct(q_shape, bf16),
            jax.ShapeDtypeStruct(q_shape, bf16),
            jax.ShapeDtypeStruct(own_shape, bf16),
            jax.ShapeDtypeStruct(far_shape, bf16),
        ),
        in_specs=[smem] + [any_space] * 4,
        out_specs=(any_space, any_space, vmem, any_space),
        scratch_shapes=[
            pltpu.VMEM(far_shape, bf16),
            dma((4,)), dma((4, heads)), dma((4, heads)), dma((peers,)), dma((peers,)),
        ],
        compiler_params=params(collective_id=0),
        name="bring",
    )(named, q_t, do_t, by_group(rotated_keys), by_group(value_vectors))

    place = jnp.stack([me, rank]).astype(jnp.int32)
    flat_lists = block_list.reshape(-1)
    ring = [[(i, (i + d) % heads) for i in range(heads)] for d in range(heads)]

    def both(at):
        return jnp.stack(
            [lax.dynamic_index_in_dim(array, at, 0, keepdims=False) for array in (q_t, do_t)]
        )

    def fetch(group, after):
        whole = jnp.zeros((2, rows * heads, width), bf16)
        for d in range(heads):
            piece = both(lax.rem(me + d, heads) * groups + group)
            if d:
                piece, _ = lax.optimization_barrier((piece, after))
                piece = lax.ppermute(piece, "head", ring[d])
            source = lax.rem(me + heads - d, heads)
            whole = lax.dynamic_update_slice(whole, piece, (0, source * rows, 0))
        return whole

    item_rows = BLOCK * per_group
    item = pl.BlockSpec((item_rows, width), lambda b, *_: (b, 0))

    def attend(group, q_spec, do_spec, q, do):
        return pl.pallas_call(
            functools.partial(attend_kernel, group, groups, run_blocks, seq_blocks),
            grid_spec=pltpu.PrefetchScalarGridSpec(
                num_scalar_prefetch=2,
                grid=(run_blocks,),
                in_specs=[
                    q_spec, do_spec,
                    pl.BlockSpec((2, 1, run_len, width), lambda b, *_: (0, group, 0, 0)),
                    pl.BlockSpec((peers, 2, 1, BLOCK, width), lambda b, *_: (0, 0, group, 0, 0)),
                ],
                out_specs=(
                    pl.BlockSpec((2, item_rows, width), lambda b, *_: (0, b, 0)),
                    pl.BlockSpec((2, run_len, width), lambda b, *_: (0, 0, 0)),
                    pl.BlockSpec((peers, 2, BLOCK, width), lambda b, *_: (0, 0, 0, 0)),
                ),
                scratch_shapes=[
                    pltpu.VMEM((TOPK * BLOCK, width), bf16),
                    pltpu.VMEM((TOPK * BLOCK, width), bf16),
                    pltpu.VMEM((2, run_len, width), jnp.float32),
                    pltpu.VMEM((peers, 2, BLOCK, width), jnp.float32),
                ],
            ),
            out_shape=(
                jax.ShapeDtypeStruct((2, rows * heads, width), bf16),
                jax.ShapeDtypeStruct((2, run_len, width), bf16),
                jax.ShapeDtypeStruct((peers, 2, BLOCK, width), bf16),
            ),
            compiler_params=pltpu.CompilerParams(
                dimension_semantics=("arbitrary",), vmem_limit_bytes=VMEM_LIMIT
            ),
            cost_estimate=pl.CostEstimate(
                flops=run_blocks * 12 * item_rows * TOPK * BLOCK * width,
                bytes_accessed=8 * rows * heads * width,
                transcendentals=run_blocks * item_rows * TOPK * BLOCK,
            ),
            name=f"attend_{group}",
        )(place, flat_lists, q, do, kv, recv)

    results = [attend(0, item, item, qh, doh)]
    both_specs = [
        pl.BlockSpec((None, item_rows, width), lambda b, *_, n=n: (n, b, 0)) for n in range(2)
    ]
    for group in range(1, groups):
        moved = fetch(group, qh)
        results.append(attend(group, *both_specs, moved, moved))
    first_out = results[0][0]
    came = []
    for d in range(heads):
        start = lax.rem(me + d, heads) * rows
        piece = lax.dynamic_slice_in_dim(first_out, start, rows, 1)
        came.append(lax.ppermute(piece, "head", ring[d]) if d else piece)

    out_g, dq_g, kv_g = pl.pallas_call(
        functools.partial(return_kernel, heads, peers, groups, run_blocks),
        out_shape=(
            jax.ShapeDtypeStruct((group_count, rows, width), bf16),
            jax.ShapeDtypeStruct((group_count, rows, width), bf16),
            jax.ShapeDtypeStruct((2, group_count, tokens, width), bf16),
        ),
        in_specs=[smem]
        + [any_space] * (heads + groups - 1)
        + [vmem] * groups
        + [any_space] * groups,
        out_specs=(any_space, any_space, any_space),
        scratch_shapes=[
            pltpu.VMEM((peers, groups, 2, BLOCK, width), bf16),
            pltpu.VMEM(own_shape, bf16),
            dma((2 * groups - 1,)), dma((2, heads)),
            dma((2 * groups - 1, heads)), dma((2 * groups - 1, heads)),
            dma((groups, peers)), dma((groups, peers)),
        ],
        compiler_params=params(collective_id=1),
        name="give_back",
    )(
        named,
        *came,
        *[result[0] for result in results[1:]],
        *[result[1] for result in results],
        *[result[2] for result in results],
    )

    def by_token(array, count):
        array = array.reshape(group_count, tokens, count, width)
        return jnp.transpose(array, (1, 0, 2, 3)).reshape(tokens, group_count * count, width)

    return (
        by_token(out_g, per_group),
        by_token(dq_g, per_group),
        by_token(kv_g[0], 1),
        by_token(kv_g[1], 1),
    )


def solution(mesh):
    split = P(("blk", "head"), None, None)
    return jax.shard_map(
        on_device,
        mesh=mesh,
        in_specs=(split, split, split, P(), split),
        out_specs=(split, split, split, split),
        check_vma=False,
    )
```

```python
import functools

import jax
import jax.numpy as jnp
from jax import lax
from jax.experimental import pallas as pl
from jax.experimental.pallas import tpu as pltpu
from jax.sharding import PartitionSpec as P

BLOCK = 128
TOPK = 8
LOG2E = 1.4426950408889634
MESH = pl.DeviceIdType.MESH
VMEM_LIMIT = 56 * 1024 * 1024


def greet(heads, peers):
    me = lax.axis_index("head")
    rank = lax.axis_index("blk")
    barrier = pltpu.get_barrier_semaphore()
    for d in range(1, heads):
        pl.semaphore_signal(
            barrier, inc=1, device_id=(lax.rem(me + d, heads), rank), device_id_type=MESH
        )
    for d in range(1, peers):
        pl.semaphore_signal(
            barrier, inc=1, device_id=(me, lax.rem(rank + d, peers)), device_id_type=MESH
        )
    pl.semaphore_wait(barrier, heads + peers - 2)
    return me, rank


def bring_kernel(
    heads, peers, groups, run_blocks,
    named, q_ref, do_ref, k_ref, v_ref,
    qh_ref, doh_ref, kv_ref, recv_ref,
    stage, own_sem, head_send, head_recv, blk_send, blk_recv,
):
    me, rank = greet(heads, peers)
    tokens = k_ref.shape[1]
    rows = q_ref.shape[1]

    def pieces(dest):
        part = pl.ds(dest * groups, groups)
        return (
            (k_ref.at[part], kv_ref.at[0, :, pl.ds(pl.multiple_of(me * tokens, 64), tokens)]),
            (v_ref.at[part], kv_ref.at[1, :, pl.ds(pl.multiple_of(me * tokens, 64), tokens)]),
            (q_ref.at[dest * groups], qh_ref.at[pl.ds(pl.multiple_of(me * rows, 128), rows)]),
            (do_ref.at[dest * groups], doh_ref.at[pl.ds(pl.multiple_of(me * rows, 128), rows)]),
        )

    remote = {}
    local = []
    for n in range(4):
        for d in range(1, heads):
            dest = lax.rem(me + d, heads)
            src, dst = pieces(dest)[n]
            copy = pltpu.make_async_remote_copy(
                src_ref=src, dst_ref=dst,
                send_sem=head_send.at[n, d], recv_sem=head_recv.at[n, d],
                device_id=(dest, rank), device_id_type=MESH,
            )
            copy.start()
            remote[n, d] = copy
        src, dst = pieces(me)[n]
        copy = pltpu.make_async_copy(src, dst, own_sem.at[n])
        copy.start()
        local.append(copy)
    for n in range(2):
        local[n].wait()
        for d in range(1, heads):
            remote[n, d].wait_recv()
    blk_copies = []
    for d in range(1, peers):
        peer = lax.rem(rank + d, peers)
        for g in range(groups):
            block = named[g * peers + peer]
            for n in range(2):
                total = jnp.zeros((BLOCK, kv_ref.shape[-1]), jnp.float32)
                for i in range(run_blocks):
                    weight = (block == i).astype(jnp.float32)
                    piece = kv_ref[n, g, i * BLOCK : (i + 1) * BLOCK, :]
                    total = total + weight * piece.astype(jnp.float32)
                stage[d, n, g] = total.astype(jnp.bfloat16)
        copy = pltpu.make_async_remote_copy(
            src_ref=stage.at[d], dst_ref=recv_ref.at[rank],
            send_sem=blk_send.at[d], recv_sem=blk_recv.at[d],
            device_id=(me, peer), device_id_type=MESH,
        )
        copy.start()
        blk_copies.append(copy)
    for n in range(2, 4):
        local[n].wait()
        for d in range(1, heads):
            remote[n, d].wait_recv()
    for copy in remote.values():
        copy.wait_send()
    for copy in blk_copies:
        copy.wait()


def attend_kernel(
    group, groups, run_blocks, seq_blocks,
    place, lists, q_ref, do_ref, kv_ref, recv_ref,
    od_ref, own_ref, far_ref,
    k_buf, v_buf, acc_own, acc_far,
):
    g, b = 0, pl.program_id(0)
    base = place[1] * run_blocks
    scale = q_ref.shape[-1] ** -0.5
    width = q_ref.shape[0] // BLOCK

    @pl.when(b == 0)
    def _():
        acc_own[...] = jnp.zeros_like(acc_own)
        acc_far[...] = jnp.zeros_like(acc_far)

    first = ((place[0] * groups + group) * seq_blocks + base + b) * TOPK
    slots = []
    for s in range(TOPK):
        listed = lists[first + s]
        mine = listed >= base
        at = jnp.clip(listed - base, 0, run_blocks - 1)
        owner = listed // run_blocks
        slots.append((listed, mine, at, owner))

        @pl.when(mine)
        def _():
            rows = pl.ds(pl.multiple_of(at * BLOCK, BLOCK), BLOCK)
            k_buf[s * BLOCK : (s + 1) * BLOCK] = kv_ref[0, g, rows, :]
            v_buf[s * BLOCK : (s + 1) * BLOCK] = kv_ref[1, g, rows, :]

        @pl.when(jnp.logical_not(mine))
        def _():
            k_buf[s * BLOCK : (s + 1) * BLOCK] = recv_ref[owner, 0, g]
            v_buf[s * BLOCK : (s + 1) * BLOCK] = recv_ref[owner, 1, g]

    q, do = q_ref[...], do_ref[...]
    keys, values = k_buf[...], v_buf[...]
    across = (((1,), (1,)), ((), ()))
    f32 = jnp.float32
    scores = lax.dot_general(keys, q, across, preferred_element_type=f32)
    shape = (BLOCK, q.shape[0])
    causal = lax.broadcasted_iota(jnp.int32, shape, 0) * width <= lax.broadcasted_iota(
        jnp.int32, shape, 1
    )
    parts = [jnp.where(causal, scores[:BLOCK], -1e30)]
    for s in range(1, TOPK):
        parts.append(
            jnp.where(slots[s][0] != base + b, scores[s * BLOCK : (s + 1) * BLOCK], -1e30)
        )
    scores = jnp.concatenate(parts, axis=0)
    top = jnp.max(scores, axis=0, keepdims=True)
    weights = jnp.exp2((scores - top) * (scale * LOG2E))
    probs = weights * (1.0 / jnp.sum(weights, axis=0, keepdims=True))
    probs_b = probs.astype(jnp.bfloat16)
    out_t = lax.dot_general(values.T, probs_b, (((1,), (0,)), ((), ())), preferred_element_type=f32)
    out_b = out_t.T.astype(jnp.bfloat16)
    od_ref[0] = out_b
    row_dot = jnp.sum(
        do.astype(f32).T * out_t.astype(jnp.bfloat16).astype(f32), axis=0, keepdims=True
    )
    grad_probs = lax.dot_general(values, do, across, preferred_element_type=f32)
    grad_scores = (probs * (grad_probs - row_dot)).astype(jnp.bfloat16)
    dq_t = lax.dot_general(
        keys.T, grad_scores, (((1,), (0,)), ((), ())), preferred_element_type=f32
    )
    od_ref[1] = (dq_t * scale).T.astype(jnp.bfloat16)
    dk = jnp.dot(grad_scores, q, preferred_element_type=f32)
    dv = jnp.dot(probs_b, do, preferred_element_type=f32)
    for s in range(TOPK):
        listed, mine, at, owner = slots[s]
        dk_s, dv_s = dk[s * BLOCK : (s + 1) * BLOCK], dv[s * BLOCK : (s + 1) * BLOCK]

        @pl.when(mine)
        def _():
            rows = pl.ds(pl.multiple_of(at * BLOCK, BLOCK), BLOCK)
            acc_own[0, rows, :] += dk_s
            acc_own[1, rows, :] += dv_s

        @pl.when(jnp.logical_not(mine))
        def _():
            acc_far[owner, 0] += dk_s
            acc_far[owner, 1] += dv_s

    @pl.when(b == run_blocks - 1)
    def _():
        own_ref[0] = (acc_own[0] * scale).astype(jnp.bfloat16)
        own_ref[1] = acc_own[1].astype(jnp.bfloat16)
        for j in range(acc_far.shape[0]):
            far_ref[j, 0] = (acc_far[j, 0] * scale).astype(jnp.bfloat16)
            far_ref[j, 1] = acc_far[j, 1].astype(jnp.bfloat16)


def return_kernel(
    heads, peers, groups, run_blocks, named, *refs,
):
    came, refs = refs[:heads], refs[heads:]
    last_refs, refs = refs[: groups - 1], refs[groups - 1 :]
    own_refs, refs = refs[:groups], refs[groups:]
    far_refs, refs = refs[:groups], refs[groups:]
    out_ref, dq_ref, kv_ref = refs[:3]
    recv, stage, own_sem, came_sem, head_send, head_recv, blk_send, blk_recv = refs[3:]
    me, rank = greet(heads, peers)
    rows = out_ref.shape[1]
    tokens = kv_ref.shape[2]
    blk_copies = []
    for d in range(1, peers):
        peer = lax.rem(rank + d, peers)
        for g in range(groups):
            copy = pltpu.make_async_remote_copy(
                src_ref=far_refs[g].at[peer], dst_ref=recv.at[rank, g],
                send_sem=blk_send.at[g, d], recv_sem=blk_recv.at[g, d],
                device_id=(me, peer), device_id_type=MESH,
            )
            copy.start()
            blk_copies.append(copy)

    def pieces(dest):
        here = pl.ds(pl.multiple_of(dest * rows, 128), rows)
        some = pl.ds(pl.multiple_of(dest * tokens, 64), tokens)
        pairs = []
        for g in range(1, groups):
            pairs.append((last_refs[g - 1].at[0, here], out_ref.at[me * groups + g]))
            pairs.append((last_refs[g - 1].at[1, here], dq_ref.at[me * groups + g]))
        pairs.append((stage.at[:, :, some], kv_ref.at[:, pl.ds(me * groups, groups)]))
        return pairs

    copies = []

    def send(n):
        for d in range(1, heads):
            dest = lax.rem(me + d, heads)
            src, dst = pieces(dest)[n]
            copy = pltpu.make_async_remote_copy(
                src_ref=src, dst_ref=dst,
                send_sem=head_send.at[n, d], recv_sem=head_recv.at[n, d],
                device_id=(dest, rank), device_id_type=MESH,
            )
            copy.start()
            copies.append(copy)
        src, dst = pieces(me)[n]
        copy = pltpu.make_async_copy(src, dst, own_sem.at[n])
        copy.start()
        copies.append(copy)

    last = 2 * (groups - 1)
    for n in range(last):
        send(n)
    for d in range(heads):
        source = lax.rem(me + heads - d, heads)
        for n, target in enumerate((out_ref, dq_ref)):
            copy = pltpu.make_async_copy(
                came[d].at[n], target.at[source * groups], came_sem.at[n, d]
            )
            copy.start()
            copies.append(copy)
    for copy in blk_copies:
        copy.wait()
    for g in range(groups):
        for n in range(2):
            def settle(i, _):
                at = pl.ds(pl.multiple_of(i * BLOCK, BLOCK), BLOCK)

                def add(d, total):
                    peer = lax.rem(rank + d, peers)
                    weight = (named[g * peers + peer] == i).astype(jnp.float32)
                    return total + weight * recv[peer, g, n].astype(jnp.float32)

                total = own_refs[g][n, at, :].astype(jnp.float32)
                total = lax.fori_loop(1, peers, add, total)
                stage[n, g, at, :] = total.astype(jnp.bfloat16)
                return 0

            lax.fori_loop(0, run_blocks, settle, 0)
    send(last)
    for copy in copies:
        copy.wait()


def on_device(queries, rotated_keys, value_vectors, block_list, grad_out):
    tokens, head_count, width = queries.shape
    group_count = rotated_keys.shape[1]
    per_group = head_count // group_count
    heads, peers = lax.axis_size("head"), lax.axis_size("blk")
    me, rank = lax.axis_index("head"), lax.axis_index("blk")
    groups = group_count // heads
    run_len = tokens * heads
    run_blocks = run_len // BLOCK
    seq_blocks = block_list.shape[1]
    rows = tokens * per_group
    bf16 = jnp.bfloat16

    def by_group(array):
        array = array.reshape(tokens, group_count, -1, width)
        return jnp.transpose(array, (1, 0, 2, 3)).reshape(group_count, -1, width)

    lists_here = lax.dynamic_slice_in_dim(block_list, me * groups, groups, 0)
    listing = lists_here.reshape(groups, peers, run_blocks * TOPK)
    inside = (listing // run_blocks == rank) & (jnp.arange(peers) != rank)[None, :, None]
    named = jnp.max(jnp.where(inside, listing - rank * run_blocks, -1), axis=2).reshape(-1)

    any_space = pl.BlockSpec(memory_space=pl.ANY)
    vmem = pl.BlockSpec(memory_space=pltpu.VMEM)
    smem = pl.BlockSpec(memory_space=pltpu.SMEM)
    dma = pltpu.SemaphoreType.DMA
    params = functools.partial(
        pltpu.CompilerParams, has_side_effects=True, vmem_limit_bytes=VMEM_LIMIT
    )
    far_shape = (peers, 2, groups, BLOCK, width)
    own_shape = (2, groups, run_len, width)
    q_shape = (rows * heads, width)
    q_t, do_t = by_group(queries), by_group(grad_out)
    qh, doh, kv, recv = pl.pallas_call(
        functools.partial(bring_kernel, heads, peers, groups, run_blocks),
        out_shape=(
            jax.ShapeDtypeStruct(q_shape, bf16),
            jax.ShapeDtypeStruct(q_shape, bf16),
            jax.ShapeDtypeStruct(own_shape, bf16),
            jax.ShapeDtypeStruct(far_shape, bf16),
        ),
        in_specs=[smem] + [any_space] * 4,
        out_specs=(any_space, any_space, vmem, any_space),
        scratch_shapes=[
            pltpu.VMEM(far_shape, bf16),
            dma((4,)), dma((4, heads)), dma((4, heads)), dma((peers,)), dma((peers,)),
        ],
        compiler_params=params(collective_id=0),
        name="bring",
    )(named, q_t, do_t, by_group(rotated_keys), by_group(value_vectors))

    place = jnp.stack([me, rank]).astype(jnp.int32)
    flat_lists = block_list.reshape(-1)
    ring = [[(i, (i + d) % heads) for i in range(heads)] for d in range(heads)]

    def both(at):
        return jnp.stack(
            [lax.dynamic_index_in_dim(array, at, 0, keepdims=False) for array in (q_t, do_t)]
        )

    def fetch(group, after):
        whole = jnp.zeros((2, rows * heads, width), bf16)
        for d in range(heads):
            piece = both(lax.rem(me + d, heads) * groups + group)
            if d:
                piece, _ = lax.optimization_barrier((piece, after))
                piece = lax.ppermute(piece, "head", ring[d])
            source = lax.rem(me + heads - d, heads)
            whole = lax.dynamic_update_slice(whole, piece, (0, source * rows, 0))
        return whole

    item_rows = BLOCK * per_group
    item = pl.BlockSpec((item_rows, width), lambda b, *_: (b, 0))

    def attend(group, q_spec, do_spec, q, do):
        return pl.pallas_call(
            functools.partial(attend_kernel, group, groups, run_blocks, seq_blocks),
            grid_spec=pltpu.PrefetchScalarGridSpec(
                num_scalar_prefetch=2,
                grid=(run_blocks,),
                in_specs=[
                    q_spec, do_spec,
                    pl.BlockSpec((2, 1, run_len, width), lambda b, *_: (0, group, 0, 0)),
                    pl.BlockSpec((peers, 2, 1, BLOCK, width), lambda b, *_: (0, 0, group, 0, 0)),
                ],
                out_specs=(
                    pl.BlockSpec((2, item_rows, width), lambda b, *_: (0, b, 0)),
                    pl.BlockSpec((2, run_len, width), lambda b, *_: (0, 0, 0)),
                    pl.BlockSpec((peers, 2, BLOCK, width), lambda b, *_: (0, 0, 0, 0)),
                ),
                scratch_shapes=[
                    pltpu.VMEM((TOPK * BLOCK, width), bf16),
                    pltpu.VMEM((TOPK * BLOCK, width), bf16),
                    pltpu.VMEM((2, run_len, width), jnp.float32),
                    pltpu.VMEM((peers, 2, BLOCK, width), jnp.float32),
                ],
            ),
            out_shape=(
                jax.ShapeDtypeStruct((2, rows * heads, width), bf16),
                jax.ShapeDtypeStruct((2, run_len, width), bf16),
                jax.ShapeDtypeStruct((peers, 2, BLOCK, width), bf16),
            ),
            compiler_params=pltpu.CompilerParams(
                dimension_semantics=("arbitrary",), vmem_limit_bytes=VMEM_LIMIT
            ),
            cost_estimate=pl.CostEstimate(
                flops=run_blocks * 12 * item_rows * TOPK * BLOCK * width,
                bytes_accessed=8 * rows * heads * width,
                transcendentals=run_blocks * item_rows * TOPK * BLOCK,
            ),
            name=f"attend_{group}",
        )(place, flat_lists, q, do, kv, recv)

    results = [attend(0, item, item, qh, doh)]
    both_specs = [
        pl.BlockSpec((None, item_rows, width), lambda b, *_, n=n: (n, b, 0)) for n in range(2)
    ]
    for group in range(1, groups):
        moved = fetch(group, qh)
        results.append(attend(group, *both_specs, moved, moved))
    first_out = results[0][0]
    came = []
    for d in range(heads):
        start = lax.rem(me + d, heads) * rows
        piece = lax.dynamic_slice_in_dim(first_out, start, rows, 1)
        came.append(lax.ppermute(piece, "head", ring[d]) if d else piece)

    out_g, dq_g, kv_g = pl.pallas_call(
        functools.partial(return_kernel, heads, peers, groups, run_blocks),
        out_shape=(
            jax.ShapeDtypeStruct((group_count, rows, width), bf16),
            jax.ShapeDtypeStruct((group_count, rows, width), bf16),
            jax.ShapeDtypeStruct((2, group_count, tokens, width), bf16),
        ),
        in_specs=[smem]
        + [vmem] * heads
        + [any_space] * (groups - 1)
        + [vmem] * groups
        + [any_space] * groups,
        out_specs=(any_space, any_space, any_space),
        scratch_shapes=[
            pltpu.VMEM((peers, groups, 2, BLOCK, width), bf16),
            pltpu.VMEM(own_shape, bf16),
            dma((2 * groups - 1,)), dma((2, heads)),
            dma((2 * groups - 1, heads)), dma((2 * groups - 1, heads)),
            dma((groups, peers)), dma((groups, peers)),
        ],
        compiler_params=params(collective_id=1),
        name="give_back",
    )(
        named,
        *came,
        *[result[0] for result in results[1:]],
        *[result[1] for result in results],
        *[result[2] for result in results],
    )

    def by_token(array, count):
        array = array.reshape(group_count, tokens, count, width)
        return jnp.transpose(array, (1, 0, 2, 3)).reshape(tokens, group_count * count, width)

    return (
        by_token(out_g, per_group),
        by_token(dq_g, per_group),
        by_token(kv_g[0], 1),
        by_token(kv_g[1], 1),
    )


def solution(mesh):
    split = P(("blk", "head"), None, None)
    return jax.shard_map(
        on_device,
        mesh=mesh,
        in_specs=(split, split, split, P(), split),
        out_specs=(split, split, split, split),
        check_vma=False,
    )
```

```python
import functools

import jax
import jax.numpy as jnp
from jax import lax
from jax.experimental import pallas as pl
from jax.experimental.pallas import tpu as pltpu
from jax.sharding import PartitionSpec as P

BLOCK = 128
TOPK = 8
LOG2E = 1.4426950408889634
MESH = pl.DeviceIdType.MESH
VMEM_LIMIT = 56 * 1024 * 1024


def greet(heads, peers):
    me = lax.axis_index("head")
    rank = lax.axis_index("blk")
    barrier = pltpu.get_barrier_semaphore()
    for d in range(1, heads):
        pl.semaphore_signal(
            barrier, inc=1, device_id=(lax.rem(me + d, heads), rank), device_id_type=MESH
        )
    for d in range(1, peers):
        pl.semaphore_signal(
            barrier, inc=1, device_id=(me, lax.rem(rank + d, peers)), device_id_type=MESH
        )
    pl.semaphore_wait(barrier, heads + peers - 2)
    return me, rank


def bring_kernel(
    heads, peers, groups, run_blocks,
    named, q_ref, do_ref, k_ref, v_ref,
    qh_ref, doh_ref, kv_ref, recv_ref,
    stage, own_sem, head_send, head_recv, blk_send, blk_recv,
):
    me, rank = greet(heads, peers)
    tokens = k_ref.shape[1]
    rows = q_ref.shape[1]

    def pieces(dest):
        part = pl.ds(dest * groups, groups)
        return (
            (k_ref.at[part], kv_ref.at[0, :, pl.ds(pl.multiple_of(me * tokens, 64), tokens)]),
            (v_ref.at[part], kv_ref.at[1, :, pl.ds(pl.multiple_of(me * tokens, 64), tokens)]),
            (q_ref.at[dest * groups], qh_ref.at[pl.ds(pl.multiple_of(me * rows, 128), rows)]),
            (do_ref.at[dest * groups], doh_ref.at[pl.ds(pl.multiple_of(me * rows, 128), rows)]),
        )

    remote = {}
    local = []
    for n in range(4):
        for d in range(1, heads):
            dest = lax.rem(me + d, heads)
            src, dst = pieces(dest)[n]
            copy = pltpu.make_async_remote_copy(
                src_ref=src, dst_ref=dst,
                send_sem=head_send.at[n, d], recv_sem=head_recv.at[n, d],
                device_id=(dest, rank), device_id_type=MESH,
            )
            copy.start()
            remote[n, d] = copy
        src, dst = pieces(me)[n]
        copy = pltpu.make_async_copy(src, dst, own_sem.at[n])
        copy.start()
        local.append(copy)
    for n in range(2):
        local[n].wait()
        for d in range(1, heads):
            remote[n, d].wait_recv()
    blk_copies = []
    for d in range(1, peers):
        peer = lax.rem(rank + d, peers)
        for g in range(groups):
            block = named[g * peers + peer]
            for n in range(2):
                total = jnp.zeros((BLOCK, kv_ref.shape[-1]), jnp.float32)
                for i in range(run_blocks):
                    weight = (block == i).astype(jnp.float32)
                    piece = kv_ref[n, g, i * BLOCK : (i + 1) * BLOCK, :]
                    total = total + weight * piece.astype(jnp.float32)
                stage[d, n, g] = total.astype(jnp.bfloat16)
        copy = pltpu.make_async_remote_copy(
            src_ref=stage.at[d], dst_ref=recv_ref.at[rank],
            send_sem=blk_send.at[d], recv_sem=blk_recv.at[d],
            device_id=(me, peer), device_id_type=MESH,
        )
        copy.start()
        blk_copies.append(copy)
    for n in range(2, 4):
        local[n].wait()
        for d in range(1, heads):
            remote[n, d].wait_recv()
    for copy in remote.values():
        copy.wait_send()
    for copy in blk_copies:
        copy.wait()


def attend_kernel(
    group, groups, run_blocks, seq_blocks,
    place, lists, q_ref, do_ref, kv_ref, recv_ref,
    od_ref, own_ref, far_ref,
    k_buf, v_buf, acc_own, acc_far,
):
    g, b = 0, pl.program_id(0)
    base = place[1] * run_blocks
    scale = q_ref.shape[-1] ** -0.5
    width = q_ref.shape[0] // BLOCK

    @pl.when(b == 0)
    def _():
        acc_own[...] = jnp.zeros_like(acc_own)
        acc_far[...] = jnp.zeros_like(acc_far)

    first = ((place[0] * groups + group) * seq_blocks + base + b) * TOPK
    slots = []
    for s in range(TOPK):
        listed = lists[first + s]
        mine = listed >= base
        at = jnp.clip(listed - base, 0, run_blocks - 1)
        owner = listed // run_blocks
        slots.append((listed, mine, at, owner))

        @pl.when(mine)
        def _():
            rows = pl.ds(pl.multiple_of(at * BLOCK, BLOCK), BLOCK)
            k_buf[s * BLOCK : (s + 1) * BLOCK] = kv_ref[0, g, rows, :]
            v_buf[s * BLOCK : (s + 1) * BLOCK] = kv_ref[1, g, rows, :]

        @pl.when(jnp.logical_not(mine))
        def _():
            k_buf[s * BLOCK : (s + 1) * BLOCK] = recv_ref[owner, 0, g]
            v_buf[s * BLOCK : (s + 1) * BLOCK] = recv_ref[owner, 1, g]

    q, do = q_ref[...], do_ref[...]
    keys, values = k_buf[...], v_buf[...]
    across = (((1,), (1,)), ((), ()))
    f32 = jnp.float32
    scores = lax.dot_general(keys, q, across, preferred_element_type=f32)
    shape = (BLOCK, q.shape[0])
    causal = lax.broadcasted_iota(jnp.int32, shape, 0) * width <= lax.broadcasted_iota(
        jnp.int32, shape, 1
    )
    parts = [jnp.where(causal, scores[:BLOCK], -1e30)]
    for s in range(1, TOPK):
        parts.append(
            jnp.where(slots[s][0] != base + b, scores[s * BLOCK : (s + 1) * BLOCK], -1e30)
        )
    scores = jnp.concatenate(parts, axis=0)
    top = jnp.max(scores, axis=0, keepdims=True)
    weights = jnp.exp2((scores - top) * (scale * LOG2E))
    probs = weights * (1.0 / jnp.sum(weights, axis=0, keepdims=True))
    probs_b = probs.astype(jnp.bfloat16)
    out_t = lax.dot_general(values.T, probs_b, (((1,), (0,)), ((), ())), preferred_element_type=f32)
    out_b = out_t.T.astype(jnp.bfloat16)
    od_ref[0] = out_b
    row_dot = jnp.sum(
        do.astype(f32).T * out_t.astype(jnp.bfloat16).astype(f32), axis=0, keepdims=True
    )
    grad_probs = lax.dot_general(values, do, across, preferred_element_type=f32)
    grad_scores = (probs * (grad_probs - row_dot)).astype(jnp.bfloat16)
    dq_t = lax.dot_general(
        keys.T, grad_scores, (((1,), (0,)), ((), ())), preferred_element_type=f32
    )
    od_ref[1] = (dq_t * scale).T.astype(jnp.bfloat16)
    dk = jnp.dot(grad_scores, q, preferred_element_type=f32)
    dv = jnp.dot(probs_b, do, preferred_element_type=f32)
    for s in range(TOPK):
        listed, mine, at, owner = slots[s]
        dk_s, dv_s = dk[s * BLOCK : (s + 1) * BLOCK], dv[s * BLOCK : (s + 1) * BLOCK]

        @pl.when(mine)
        def _():
            rows = pl.ds(pl.multiple_of(at * BLOCK, BLOCK), BLOCK)
            acc_own[0, rows, :] += dk_s
            acc_own[1, rows, :] += dv_s

        @pl.when(jnp.logical_not(mine))
        def _():
            acc_far[owner, 0] += dk_s
            acc_far[owner, 1] += dv_s

    @pl.when(b == run_blocks - 1)
    def _():
        own_ref[0] = (acc_own[0] * scale).astype(jnp.bfloat16)
        own_ref[1] = acc_own[1].astype(jnp.bfloat16)
        for j in range(acc_far.shape[0]):
            far_ref[j, 0] = (acc_far[j, 0] * scale).astype(jnp.bfloat16)
            far_ref[j, 1] = acc_far[j, 1].astype(jnp.bfloat16)


def return_kernel(
    heads, peers, groups, run_blocks, named, *refs,
):
    came, refs = refs[:heads], refs[heads:]
    last_refs, refs = refs[: groups - 1], refs[groups - 1 :]
    own_refs, refs = refs[:groups], refs[groups:]
    far_refs, refs = refs[:groups], refs[groups:]
    out_ref, dq_ref, kv_ref = refs[:3]
    recv, stage, own_sem, came_sem, head_send, head_recv, blk_send, blk_recv = refs[3:]
    me, rank = greet(heads, peers)
    rows = out_ref.shape[1]
    tokens = kv_ref.shape[2]
    blk_copies = []
    for g in range(groups):
        for d in range(1, peers):
            peer = lax.rem(rank + d, peers)
            copy = pltpu.make_async_remote_copy(
                src_ref=far_refs[g].at[peer], dst_ref=recv.at[rank, g],
                send_sem=blk_send.at[g, d], recv_sem=blk_recv.at[g, d],
                device_id=(me, peer), device_id_type=MESH,
            )
            copy.start()
            blk_copies.append(copy)

    def pieces(dest):
        here = pl.ds(pl.multiple_of(dest * rows, 128), rows)
        some = pl.ds(pl.multiple_of(dest * tokens, 64), tokens)
        pairs = []
        for g in range(1, groups):
            pairs.append((last_refs[g - 1].at[0, here], out_ref.at[me * groups + g]))
            pairs.append((last_refs[g - 1].at[1, here], dq_ref.at[me * groups + g]))
        for g in range(groups):
            pairs.append((stage.at[:, g, some], kv_ref.at[:, me * groups + g]))
        return pairs

    copies = []

    def send(n):
        for d in range(1, heads):
            dest = lax.rem(me + d, heads)
            src, dst = pieces(dest)[n]
            copy = pltpu.make_async_remote_copy(
                src_ref=src, dst_ref=dst,
                send_sem=head_send.at[n, d], recv_sem=head_recv.at[n, d],
                device_id=(dest, rank), device_id_type=MESH,
            )
            copy.start()
            copies.append(copy)
        src, dst = pieces(me)[n]
        copy = pltpu.make_async_copy(src, dst, own_sem.at[n])
        copy.start()
        copies.append(copy)

    last = 2 * (groups - 1)
    for n in range(last):
        send(n)
    for d in range(heads):
        source = lax.rem(me + heads - d, heads)
        for n, target in enumerate((out_ref, dq_ref)):
            copy = pltpu.make_async_copy(
                came[d].at[n], target.at[source * groups], came_sem.at[n, d]
            )
            copy.start()
            copies.append(copy)
    for g in range(groups):
        for copy in blk_copies[g * (peers - 1) : (g + 1) * (peers - 1)]:
            copy.wait_recv()
        for n in range(2):
            def settle(i, _):
                at = pl.ds(pl.multiple_of(i * BLOCK, BLOCK), BLOCK)

                def add(d, total):
                    peer = lax.rem(rank + d, peers)
                    weight = (named[g * peers + peer] == i).astype(jnp.float32)
                    return total + weight * recv[peer, g, n].astype(jnp.float32)

                total = own_refs[g][n, at, :].astype(jnp.float32)
                total = lax.fori_loop(1, peers, add, total)
                stage[n, g, at, :] = total.astype(jnp.bfloat16)
                return 0

            lax.fori_loop(0, run_blocks, settle, 0)
        send(last + g)
    for copy in blk_copies:
        copy.wait_send()
    for copy in copies:
        copy.wait()


def on_device(queries, rotated_keys, value_vectors, block_list, grad_out):
    tokens, head_count, width = queries.shape
    group_count = rotated_keys.shape[1]
    per_group = head_count // group_count
    heads, peers = lax.axis_size("head"), lax.axis_size("blk")
    me, rank = lax.axis_index("head"), lax.axis_index("blk")
    groups = group_count // heads
    run_len = tokens * heads
    run_blocks = run_len // BLOCK
    seq_blocks = block_list.shape[1]
    rows = tokens * per_group
    bf16 = jnp.bfloat16

    def by_group(array):
        array = array.reshape(tokens, group_count, -1, width)
        return jnp.transpose(array, (1, 0, 2, 3)).reshape(group_count, -1, width)

    lists_here = lax.dynamic_slice_in_dim(block_list, me * groups, groups, 0)
    listing = lists_here.reshape(groups, peers, run_blocks * TOPK)
    inside = (listing // run_blocks == rank) & (jnp.arange(peers) != rank)[None, :, None]
    named = jnp.max(jnp.where(inside, listing - rank * run_blocks, -1), axis=2).reshape(-1)

    any_space = pl.BlockSpec(memory_space=pl.ANY)
    vmem = pl.BlockSpec(memory_space=pltpu.VMEM)
    smem = pl.BlockSpec(memory_space=pltpu.SMEM)
    dma = pltpu.SemaphoreType.DMA
    params = functools.partial(
        pltpu.CompilerParams, has_side_effects=True, vmem_limit_bytes=VMEM_LIMIT
    )
    far_shape = (peers, 2, groups, BLOCK, width)
    own_shape = (2, groups, run_len, width)
    q_shape = (rows * heads, width)
    q_t, do_t = by_group(queries), by_group(grad_out)
    qh, doh, kv, recv = pl.pallas_call(
        functools.partial(bring_kernel, heads, peers, groups, run_blocks),
        out_shape=(
            jax.ShapeDtypeStruct(q_shape, bf16),
            jax.ShapeDtypeStruct(q_shape, bf16),
            jax.ShapeDtypeStruct(own_shape, bf16),
            jax.ShapeDtypeStruct(far_shape, bf16),
        ),
        in_specs=[smem] + [any_space] * 4,
        out_specs=(any_space, any_space, vmem, any_space),
        scratch_shapes=[
            pltpu.VMEM(far_shape, bf16),
            dma((4,)), dma((4, heads)), dma((4, heads)), dma((peers,)), dma((peers,)),
        ],
        compiler_params=params(collective_id=0),
        name="bring",
    )(named, q_t, do_t, by_group(rotated_keys), by_group(value_vectors))

    place = jnp.stack([me, rank]).astype(jnp.int32)
    flat_lists = block_list.reshape(-1)
    ring = [[(i, (i + d) % heads) for i in range(heads)] for d in range(heads)]

    def both(at):
        return jnp.stack(
            [lax.dynamic_index_in_dim(array, at, 0, keepdims=False) for array in (q_t, do_t)]
        )

    def fetch(group, after):
        whole = jnp.zeros((2, rows * heads, width), bf16)
        for d in range(heads):
            piece = both(lax.rem(me + d, heads) * groups + group)
            if d:
                piece, _ = lax.optimization_barrier((piece, after))
                piece = lax.ppermute(piece, "head", ring[d])
            source = lax.rem(me + heads - d, heads)
            whole = lax.dynamic_update_slice(whole, piece, (0, source * rows, 0))
        return whole

    item_rows = BLOCK * per_group
    item = pl.BlockSpec((item_rows, width), lambda b, *_: (b, 0))

    def attend(group, q_spec, do_spec, q, do):
        return pl.pallas_call(
            functools.partial(attend_kernel, group, groups, run_blocks, seq_blocks),
            grid_spec=pltpu.PrefetchScalarGridSpec(
                num_scalar_prefetch=2,
                grid=(run_blocks,),
                in_specs=[
                    q_spec, do_spec,
                    pl.BlockSpec((2, 1, run_len, width), lambda b, *_: (0, group, 0, 0)),
                    pl.BlockSpec((peers, 2, 1, BLOCK, width), lambda b, *_: (0, 0, group, 0, 0)),
                ],
                out_specs=(
                    pl.BlockSpec((2, item_rows, width), lambda b, *_: (0, b, 0)),
                    pl.BlockSpec((2, run_len, width), lambda b, *_: (0, 0, 0)),
                    pl.BlockSpec((peers, 2, BLOCK, width), lambda b, *_: (0, 0, 0, 0)),
                ),
                scratch_shapes=[
                    pltpu.VMEM((TOPK * BLOCK, width), bf16),
                    pltpu.VMEM((TOPK * BLOCK, width), bf16),
                    pltpu.VMEM((2, run_len, width), jnp.float32),
                    pltpu.VMEM((peers, 2, BLOCK, width), jnp.float32),
                ],
            ),
            out_shape=(
                jax.ShapeDtypeStruct((2, rows * heads, width), bf16),
                jax.ShapeDtypeStruct((2, run_len, width), bf16),
                jax.ShapeDtypeStruct((peers, 2, BLOCK, width), bf16),
            ),
            compiler_params=pltpu.CompilerParams(
                dimension_semantics=("arbitrary",), vmem_limit_bytes=VMEM_LIMIT
            ),
            cost_estimate=pl.CostEstimate(
                flops=run_blocks * 12 * item_rows * TOPK * BLOCK * width,
                bytes_accessed=8 * rows * heads * width,
                transcendentals=run_blocks * item_rows * TOPK * BLOCK,
            ),
            name=f"attend_{group}",
        )(place, flat_lists, q, do, kv, recv)

    results = [attend(0, item, item, qh, doh)]
    both_specs = [
        pl.BlockSpec((None, item_rows, width), lambda b, *_, n=n: (n, b, 0)) for n in range(2)
    ]
    for group in range(1, groups):
        moved = fetch(group, qh)
        results.append(attend(group, *both_specs, moved, moved))
    first_out = results[0][0]
    came = []
    for d in range(heads):
        start = lax.rem(me + d, heads) * rows
        piece = lax.dynamic_slice_in_dim(first_out, start, rows, 1)
        came.append(lax.ppermute(piece, "head", ring[d]) if d else piece)

    out_g, dq_g, kv_g = pl.pallas_call(
        functools.partial(return_kernel, heads, peers, groups, run_blocks),
        out_shape=(
            jax.ShapeDtypeStruct((group_count, rows, width), bf16),
            jax.ShapeDtypeStruct((group_count, rows, width), bf16),
            jax.ShapeDtypeStruct((2, group_count, tokens, width), bf16),
        ),
        in_specs=[smem]
        + [vmem] * heads
        + [any_space] * (groups - 1)
        + [vmem] * groups
        + [any_space] * groups,
        out_specs=(any_space, any_space, any_space),
        scratch_shapes=[
            pltpu.VMEM((peers, groups, 2, BLOCK, width), bf16),
            pltpu.VMEM(own_shape, bf16),
            dma((3 * groups - 2,)), dma((2, heads)),
            dma((3 * groups - 2, heads)), dma((3 * groups - 2, heads)),
            dma((groups, peers)), dma((groups, peers)),
        ],
        compiler_params=params(collective_id=1),
        name="give_back",
    )(
        named,
        *came,
        *[result[0] for result in results[1:]],
        *[result[1] for result in results],
        *[result[2] for result in results],
    )

    def by_token(array, count):
        array = array.reshape(group_count, tokens, count, width)
        return jnp.transpose(array, (1, 0, 2, 3)).reshape(tokens, group_count * count, width)

    return (
        by_token(out_g, per_group),
        by_token(dq_g, per_group),
        by_token(kv_g[0], 1),
        by_token(kv_g[1], 1),
    )


def solution(mesh):
    split = P(("blk", "head"), None, None)
    return jax.shard_map(
        on_device,
        mesh=mesh,
        in_specs=(split, split, split, P(), split),
        out_specs=(split, split, split, split),
        check_vma=False,
    )
```

```python
import functools

import jax
import jax.numpy as jnp
from jax import lax
from jax.experimental import pallas as pl
from jax.experimental.pallas import tpu as pltpu
from jax.sharding import PartitionSpec as P

BLOCK = 128
TOPK = 8
LOG2E = 1.4426950408889634
MESH = pl.DeviceIdType.MESH
VMEM_LIMIT = 56 * 1024 * 1024


def greet(heads, peers):
    me = lax.axis_index("head")
    rank = lax.axis_index("blk")
    barrier = pltpu.get_barrier_semaphore()
    for d in range(1, heads):
        pl.semaphore_signal(
            barrier, inc=1, device_id=(lax.rem(me + d, heads), rank), device_id_type=MESH
        )
    for d in range(1, peers):
        pl.semaphore_signal(
            barrier, inc=1, device_id=(me, lax.rem(rank + d, peers)), device_id_type=MESH
        )
    pl.semaphore_wait(barrier, heads + peers - 2)
    return me, rank


def bring_kernel(
    heads, peers, groups, run_blocks,
    named, q_ref, do_ref, k_ref, v_ref,
    qh_ref, doh_ref, kv_ref, recv_ref,
    stage, own_sem, head_send, head_recv, blk_send, blk_recv,
):
    me, rank = greet(heads, peers)
    tokens = k_ref.shape[1]
    rows = q_ref.shape[1]

    def pieces(dest):
        here = pl.ds(pl.multiple_of(me * tokens, 64), tokens)
        pairs = []
        for g in range(groups):
            pairs.append((k_ref.at[dest * groups + g], kv_ref.at[0, g, here]))
            pairs.append((v_ref.at[dest * groups + g], kv_ref.at[1, g, here]))
        return pairs + [
            (q_ref.at[dest * groups], qh_ref.at[pl.ds(pl.multiple_of(me * rows, 128), rows)]),
            (do_ref.at[dest * groups], doh_ref.at[pl.ds(pl.multiple_of(me * rows, 128), rows)]),
        ]

    remote = {}
    local = []
    for n in range(2 * groups + 2):
        for d in range(1, heads):
            dest = lax.rem(me + d, heads)
            src, dst = pieces(dest)[n]
            copy = pltpu.make_async_remote_copy(
                src_ref=src, dst_ref=dst,
                send_sem=head_send.at[n, d], recv_sem=head_recv.at[n, d],
                device_id=(dest, rank), device_id_type=MESH,
            )
            copy.start()
            remote[n, d] = copy
        src, dst = pieces(me)[n]
        copy = pltpu.make_async_copy(src, dst, own_sem.at[n])
        copy.start()
        local.append(copy)
    blk_copies = []
    for g in range(groups):
        for n in (2 * g, 2 * g + 1):
            local[n].wait()
            for d in range(1, heads):
                remote[n, d].wait_recv()
        for d in range(1, peers):
            peer = lax.rem(rank + d, peers)
            block = named[g * peers + peer]
            for n in range(2):
                total = jnp.zeros((BLOCK, kv_ref.shape[-1]), jnp.float32)
                for i in range(run_blocks):
                    weight = (block == i).astype(jnp.float32)
                    piece = kv_ref[n, g, i * BLOCK : (i + 1) * BLOCK, :]
                    total = total + weight * piece.astype(jnp.float32)
                stage[d, n, g] = total.astype(jnp.bfloat16)
            copy = pltpu.make_async_remote_copy(
                src_ref=stage.at[d, :, g], dst_ref=recv_ref.at[rank, :, g],
                send_sem=blk_send.at[g, d], recv_sem=blk_recv.at[g, d],
                device_id=(me, peer), device_id_type=MESH,
            )
            copy.start()
            blk_copies.append(copy)
    for n in range(2 * groups, 2 * groups + 2):
        local[n].wait()
        for d in range(1, heads):
            remote[n, d].wait_recv()
    for copy in remote.values():
        copy.wait_send()
    for copy in blk_copies:
        copy.wait()


def attend_kernel(
    group, groups, run_blocks, seq_blocks,
    place, lists, q_ref, do_ref, kv_ref, recv_ref,
    od_ref, own_ref, far_ref,
    k_buf, v_buf, acc_own, acc_far,
):
    g, b = 0, pl.program_id(0)
    base = place[1] * run_blocks
    scale = q_ref.shape[-1] ** -0.5
    width = q_ref.shape[0] // BLOCK

    @pl.when(b == 0)
    def _():
        acc_own[...] = jnp.zeros_like(acc_own)
        acc_far[...] = jnp.zeros_like(acc_far)

    first = ((place[0] * groups + group) * seq_blocks + base + b) * TOPK
    slots = []
    for s in range(TOPK):
        listed = lists[first + s]
        mine = listed >= base
        at = jnp.clip(listed - base, 0, run_blocks - 1)
        owner = listed // run_blocks
        slots.append((listed, mine, at, owner))

        @pl.when(mine)
        def _():
            rows = pl.ds(pl.multiple_of(at * BLOCK, BLOCK), BLOCK)
            k_buf[s * BLOCK : (s + 1) * BLOCK] = kv_ref[0, g, rows, :]
            v_buf[s * BLOCK : (s + 1) * BLOCK] = kv_ref[1, g, rows, :]

        @pl.when(jnp.logical_not(mine))
        def _():
            k_buf[s * BLOCK : (s + 1) * BLOCK] = recv_ref[owner, 0, g]
            v_buf[s * BLOCK : (s + 1) * BLOCK] = recv_ref[owner, 1, g]

    q, do = q_ref[...], do_ref[...]
    keys, values = k_buf[...], v_buf[...]
    across = (((1,), (1,)), ((), ()))
    f32 = jnp.float32
    scores = lax.dot_general(keys, q, across, preferred_element_type=f32)
    shape = (BLOCK, q.shape[0])
    causal = lax.broadcasted_iota(jnp.int32, shape, 0) * width <= lax.broadcasted_iota(
        jnp.int32, shape, 1
    )
    parts = [jnp.where(causal, scores[:BLOCK], -1e30)]
    for s in range(1, TOPK):
        parts.append(
            jnp.where(slots[s][0] != base + b, scores[s * BLOCK : (s + 1) * BLOCK], -1e30)
        )
    scores = jnp.concatenate(parts, axis=0)
    top = jnp.max(scores, axis=0, keepdims=True)
    weights = jnp.exp2((scores - top) * (scale * LOG2E))
    probs = weights * (1.0 / jnp.sum(weights, axis=0, keepdims=True))
    probs_b = probs.astype(jnp.bfloat16)
    out_t = lax.dot_general(values.T, probs_b, (((1,), (0,)), ((), ())), preferred_element_type=f32)
    out_b = out_t.T.astype(jnp.bfloat16)
    od_ref[0] = out_b
    row_dot = jnp.sum(
        do.astype(f32).T * out_t.astype(jnp.bfloat16).astype(f32), axis=0, keepdims=True
    )
    grad_probs = lax.dot_general(values, do, across, preferred_element_type=f32)
    grad_scores = (probs * (grad_probs - row_dot)).astype(jnp.bfloat16)
    dq_t = lax.dot_general(
        keys.T, grad_scores, (((1,), (0,)), ((), ())), preferred_element_type=f32
    )
    od_ref[1] = (dq_t * scale).T.astype(jnp.bfloat16)
    dk = jnp.dot(grad_scores, q, preferred_element_type=f32)
    dv = jnp.dot(probs_b, do, preferred_element_type=f32)
    for s in range(TOPK):
        listed, mine, at, owner = slots[s]
        dk_s, dv_s = dk[s * BLOCK : (s + 1) * BLOCK], dv[s * BLOCK : (s + 1) * BLOCK]

        @pl.when(mine)
        def _():
            rows = pl.ds(pl.multiple_of(at * BLOCK, BLOCK), BLOCK)
            acc_own[0, rows, :] += dk_s
            acc_own[1, rows, :] += dv_s

        @pl.when(jnp.logical_not(mine))
        def _():
            acc_far[owner, 0] += dk_s
            acc_far[owner, 1] += dv_s

    @pl.when(b == run_blocks - 1)
    def _():
        own_ref[0] = (acc_own[0] * scale).astype(jnp.bfloat16)
        own_ref[1] = acc_own[1].astype(jnp.bfloat16)
        for j in range(acc_far.shape[0]):
            far_ref[j, 0] = (acc_far[j, 0] * scale).astype(jnp.bfloat16)
            far_ref[j, 1] = acc_far[j, 1].astype(jnp.bfloat16)


def return_kernel(
    heads, peers, groups, run_blocks, named, *refs,
):
    came, refs = refs[:heads], refs[heads:]
    last_refs, refs = refs[: groups - 1], refs[groups - 1 :]
    own_refs, refs = refs[:groups], refs[groups:]
    far_refs, refs = refs[:groups], refs[groups:]
    out_ref, dq_ref, kv_ref = refs[:3]
    recv, stage, own_sem, came_sem, head_send, head_recv, blk_send, blk_recv = refs[3:]
    me, rank = greet(heads, peers)
    rows = out_ref.shape[1]
    tokens = kv_ref.shape[2]
    blk_copies = []
    for g in range(groups):
        for d in range(1, peers):
            peer = lax.rem(rank + d, peers)
            copy = pltpu.make_async_remote_copy(
                src_ref=far_refs[g].at[peer], dst_ref=recv.at[rank, g],
                send_sem=blk_send.at[g, d], recv_sem=blk_recv.at[g, d],
                device_id=(me, peer), device_id_type=MESH,
            )
            copy.start()
            blk_copies.append(copy)

    def pieces(dest):
        here = pl.ds(pl.multiple_of(dest * rows, 128), rows)
        some = pl.ds(pl.multiple_of(dest * tokens, 64), tokens)
        pairs = []
        for g in range(1, groups):
            pairs.append((last_refs[g - 1].at[0, here], out_ref.at[me * groups + g]))
            pairs.append((last_refs[g - 1].at[1, here], dq_ref.at[me * groups + g]))
        for g in range(groups):
            pairs.append((stage.at[:, g, some], kv_ref.at[:, me * groups + g]))
        return pairs

    copies = []

    def send(n):
        for d in range(1, heads):
            dest = lax.rem(me + d, heads)
            src, dst = pieces(dest)[n]
            copy = pltpu.make_async_remote_copy(
                src_ref=src, dst_ref=dst,
                send_sem=head_send.at[n, d], recv_sem=head_recv.at[n, d],
                device_id=(dest, rank), device_id_type=MESH,
            )
            copy.start()
            copies.append(copy)
        src, dst = pieces(me)[n]
        copy = pltpu.make_async_copy(src, dst, own_sem.at[n])
        copy.start()
        copies.append(copy)

    last = 2 * (groups - 1)
    for n in range(last):
        send(n)
    for d in range(heads):
        source = lax.rem(me + heads - d, heads)
        for n, target in enumerate((out_ref, dq_ref)):
            copy = pltpu.make_async_copy(
                came[d].at[n], target.at[source * groups], came_sem.at[n, d]
            )
            copy.start()
            copies.append(copy)
    for g in range(groups):
        for copy in blk_copies[g * (peers - 1) : (g + 1) * (peers - 1)]:
            copy.wait_recv()
        for n in range(2):
            def settle(i, _):
                at = pl.ds(pl.multiple_of(i * BLOCK, BLOCK), BLOCK)

                def add(d, total):
                    peer = lax.rem(rank + d, peers)
                    weight = (named[g * peers + peer] == i).astype(jnp.float32)
                    return total + weight * recv[peer, g, n].astype(jnp.float32)

                total = own_refs[g][n, at, :].astype(jnp.float32)
                total = lax.fori_loop(1, peers, add, total)
                stage[n, g, at, :] = total.astype(jnp.bfloat16)
                return 0

            lax.fori_loop(0, run_blocks, settle, 0)
        send(last + g)
    for copy in blk_copies:
        copy.wait_send()
    for copy in copies:
        copy.wait()


def on_device(queries, rotated_keys, value_vectors, block_list, grad_out):
    tokens, head_count, width = queries.shape
    group_count = rotated_keys.shape[1]
    per_group = head_count // group_count
    heads, peers = lax.axis_size("head"), lax.axis_size("blk")
    me, rank = lax.axis_index("head"), lax.axis_index("blk")
    groups = group_count // heads
    run_len = tokens * heads
    run_blocks = run_len // BLOCK
    seq_blocks = block_list.shape[1]
    rows = tokens * per_group
    bf16 = jnp.bfloat16

    def by_group(array):
        array = array.reshape(tokens, group_count, -1, width)
        return jnp.transpose(array, (1, 0, 2, 3)).reshape(group_count, -1, width)

    lists_here = lax.dynamic_slice_in_dim(block_list, me * groups, groups, 0)
    listing = lists_here.reshape(groups, peers, run_blocks * TOPK)
    inside = (listing // run_blocks == rank) & (jnp.arange(peers) != rank)[None, :, None]
    named = jnp.max(jnp.where(inside, listing - rank * run_blocks, -1), axis=2).reshape(-1)

    any_space = pl.BlockSpec(memory_space=pl.ANY)
    vmem = pl.BlockSpec(memory_space=pltpu.VMEM)
    smem = pl.BlockSpec(memory_space=pltpu.SMEM)
    dma = pltpu.SemaphoreType.DMA
    params = functools.partial(
        pltpu.CompilerParams, has_side_effects=True, vmem_limit_bytes=VMEM_LIMIT
    )
    far_shape = (peers, 2, groups, BLOCK, width)
    own_shape = (2, groups, run_len, width)
    q_shape = (rows * heads, width)
    q_t, do_t = by_group(queries), by_group(grad_out)
    qh, doh, kv, recv = pl.pallas_call(
        functools.partial(bring_kernel, heads, peers, groups, run_blocks),
        out_shape=(
            jax.ShapeDtypeStruct(q_shape, bf16),
            jax.ShapeDtypeStruct(q_shape, bf16),
            jax.ShapeDtypeStruct(own_shape, bf16),
            jax.ShapeDtypeStruct(far_shape, bf16),
        ),
        in_specs=[smem] + [any_space] * 4,
        out_specs=(any_space, any_space, vmem, any_space),
        scratch_shapes=[
            pltpu.VMEM(far_shape, bf16),
            dma((2 * groups + 2,)), dma((2 * groups + 2, heads)), dma((2 * groups + 2, heads)),
            dma((groups, peers)), dma((groups, peers)),
        ],
        compiler_params=params(collective_id=0),
        name="bring",
    )(named, q_t, do_t, by_group(rotated_keys), by_group(value_vectors))

    place = jnp.stack([me, rank]).astype(jnp.int32)
    flat_lists = block_list.reshape(-1)
    ring = [[(i, (i + d) % heads) for i in range(heads)] for d in range(heads)]

    def both(at):
        return jnp.stack(
            [lax.dynamic_index_in_dim(array, at, 0, keepdims=False) for array in (q_t, do_t)]
        )

    def fetch(group, after):
        whole = jnp.zeros((2, rows * heads, width), bf16)
        for d in range(heads):
            piece = both(lax.rem(me + d, heads) * groups + group)
            if d:
                piece, _ = lax.optimization_barrier((piece, after))
                piece = lax.ppermute(piece, "head", ring[d])
            source = lax.rem(me + heads - d, heads)
            whole = lax.dynamic_update_slice(whole, piece, (0, source * rows, 0))
        return whole

    item_rows = BLOCK * per_group
    item = pl.BlockSpec((item_rows, width), lambda b, *_: (b, 0))

    def attend(group, q_spec, do_spec, q, do):
        return pl.pallas_call(
            functools.partial(attend_kernel, group, groups, run_blocks, seq_blocks),
            grid_spec=pltpu.PrefetchScalarGridSpec(
                num_scalar_prefetch=2,
                grid=(run_blocks,),
                in_specs=[
                    q_spec, do_spec,
                    pl.BlockSpec((2, 1, run_len, width), lambda b, *_: (0, group, 0, 0)),
                    pl.BlockSpec((peers, 2, 1, BLOCK, width), lambda b, *_: (0, 0, group, 0, 0)),
                ],
                out_specs=(
                    pl.BlockSpec((2, item_rows, width), lambda b, *_: (0, b, 0)),
                    pl.BlockSpec((2, run_len, width), lambda b, *_: (0, 0, 0)),
                    pl.BlockSpec((peers, 2, BLOCK, width), lambda b, *_: (0, 0, 0, 0)),
                ),
                scratch_shapes=[
                    pltpu.VMEM((TOPK * BLOCK, width), bf16),
                    pltpu.VMEM((TOPK * BLOCK, width), bf16),
                    pltpu.VMEM((2, run_len, width), jnp.float32),
                    pltpu.VMEM((peers, 2, BLOCK, width), jnp.float32),
                ],
            ),
            out_shape=(
                jax.ShapeDtypeStruct((2, rows * heads, width), bf16),
                jax.ShapeDtypeStruct((2, run_len, width), bf16),
                jax.ShapeDtypeStruct((peers, 2, BLOCK, width), bf16),
            ),
            compiler_params=pltpu.CompilerParams(
                dimension_semantics=("arbitrary",), vmem_limit_bytes=VMEM_LIMIT
            ),
            cost_estimate=pl.CostEstimate(
                flops=run_blocks * 12 * item_rows * TOPK * BLOCK * width,
                bytes_accessed=8 * rows * heads * width,
                transcendentals=run_blocks * item_rows * TOPK * BLOCK,
            ),
            name=f"attend_{group}",
        )(place, flat_lists, q, do, kv, recv)

    results = [attend(0, item, item, qh, doh)]
    both_specs = [
        pl.BlockSpec((None, item_rows, width), lambda b, *_, n=n: (n, b, 0)) for n in range(2)
    ]
    for group in range(1, groups):
        moved = fetch(group, qh)
        results.append(attend(group, *both_specs, moved, moved))
    first_out = results[0][0]
    came = []
    for d in range(heads):
        start = lax.rem(me + d, heads) * rows
        piece = lax.dynamic_slice_in_dim(first_out, start, rows, 1)
        came.append(lax.ppermute(piece, "head", ring[d]) if d else piece)

    out_g, dq_g, kv_g = pl.pallas_call(
        functools.partial(return_kernel, heads, peers, groups, run_blocks),
        out_shape=(
            jax.ShapeDtypeStruct((group_count, rows, width), bf16),
            jax.ShapeDtypeStruct((group_count, rows, width), bf16),
            jax.ShapeDtypeStruct((2, group_count, tokens, width), bf16),
        ),
        in_specs=[smem]
        + [vmem] * heads
        + [any_space] * (groups - 1)
        + [vmem] * groups
        + [any_space] * groups,
        out_specs=(any_space, any_space, any_space),
        scratch_shapes=[
            pltpu.VMEM((peers, groups, 2, BLOCK, width), bf16),
            pltpu.VMEM(own_shape, bf16),
            dma((3 * groups - 2,)), dma((2, heads)),
            dma((3 * groups - 2, heads)), dma((3 * groups - 2, heads)),
            dma((groups, peers)), dma((groups, peers)),
        ],
        compiler_params=params(collective_id=1),
        name="give_back",
    )(
        named,
        *came,
        *[result[0] for result in results[1:]],
        *[result[1] for result in results],
        *[result[2] for result in results],
    )

    def by_token(array, count):
        array = array.reshape(group_count, tokens, count, width)
        return jnp.transpose(array, (1, 0, 2, 3)).reshape(tokens, group_count * count, width)

    return (
        by_token(out_g, per_group),
        by_token(dq_g, per_group),
        by_token(kv_g[0], 1),
        by_token(kv_g[1], 1),
    )


def solution(mesh):
    split = P(("blk", "head"), None, None)
    return jax.shard_map(
        on_device,
        mesh=mesh,
        in_specs=(split, split, split, P(), split),
        out_specs=(split, split, split, split),
        check_vma=False,
    )
```
